512 devices in a mesh: dp: 32 (over y, x_hi, core), ctx: 16 (over z, x_lo).
Axes of the slice: x: 4 (x_hi: 2, x_lo: 2; x = x_hi * 2 + x_lo), y: 8, z: 8, core: 2. Of those that a mesh axis runs over, the one named last changes fastest.
Arguments:
- queries: bfloat16 [32, 2048, 1536], P('dp', 'ctx'), may hold values from -5 to 5
- keys: bfloat16 [32, 2048, 1536], P('dp', 'ctx'), may hold values from -5 to 5
- values: bfloat16 [32, 2048, 1536], P('dp', 'ctx'), may hold values from -6 to 6
- grad_out: bfloat16 [32, 2048, 1536], P('dp', 'ctx'), may hold values from -6 to 6
- clip_tokens: int32 [32], replicated, may hold values from 896 to 1792, as said below
- text_tokens: int32 [32], replicated, may hold values from 64 to 256, as said below
- anchor_rank: int32 [32, 16, 32], P('dp', 'ctx'), may hold values from 0 to 31, each once within a row
- send_block: int32 [32, 16, 32], P('dp', 'ctx'), may hold values from 0 to 31, each once within a row
Outputs:
- attended: bfloat16 [32, 2048, 1536], P('dp', 'ctx')
- query_grad: bfloat16 [32, 2048, 1536], P('dp', 'ctx')
The draws below stay inside these ranges and needn't reach their ends.
Inputs may be any that keep to these rules, and one draw needn't show every extreme that they name: `clip_tokens`: some clip has exactly 1792 latent tokens in every draw. `text_tokens`: some clip has exactly 256 text tokens in every draw. anchor_rank[e, c, :] is a permutation of 0 to 31. send_block[d, c, :] is a permutation of 0 to 31.
All inputs are finite; a program needn't handle non-finite values.
Results may differ from the reference program's by a relative error of at most 0.011.
Values may be sent and summed in bfloat16 or wider, within the bound.
A program may use at most 128 MiB of HBM per device.

```python
import jax
import jax.numpy as jnp
from jax import lax

H = 12
DH = 128
TEXT = 256
TOK_DEV = 128
CLIPS = 32
SEQ = 2048
MOVE = 4
N_CTX = 16


def draw_queries(key, part):
    key = jax.random.fold_in(key, 11)
    return jnp.clip(1.6 * jax.random.normal(key, (CLIPS, SEQ, H * DH), jnp.float32), -5.0, 5.0).astype(jnp.bfloat16)


def draw_keys(key, part):
    key = jax.random.fold_in(key, 23)
    return jnp.clip(1.6 * jax.random.normal(key, (CLIPS, SEQ, H * DH), jnp.float32), -5.0, 5.0).astype(jnp.bfloat16)


def reach_top(key, lowest, highest):
    value_key, where_key = jax.random.split(key)
    picked = jax.random.randint(value_key, (CLIPS,), lowest, highest + 1)
    where_top = jax.random.randint(where_key, (), 0, CLIPS)
    return jnp.where(jnp.arange(CLIPS) == where_top, highest, picked).astype(jnp.int32)


def draw_clip_tokens(key, part):
    key = jax.random.fold_in(key, 37)
    return reach_top(key, (SEQ - TEXT) // 2, SEQ - TEXT)


def draw_text_tokens(key, part):
    key = jax.random.fold_in(key, 41)
    return reach_top(key, TEXT // 4, TEXT)


def block_scale(rng, shape, cuts, smallest, largest):
    level = 1.0
    for axis_at, shards_of in cuts:
        steps = jax.random.uniform(jax.random.fold_in(jax.random.fold_in(rng, 6), axis_at), (shards_of,), jnp.float32, smallest / len(cuts), largest / len(cuts))
        level = level * jnp.repeat(jnp.exp(steps), shape[axis_at] // shards_of).reshape((-1,) + (1,) * (len(shape) - 1 - axis_at))
    return level


def normal_values(key, shape, deviation, reach, cuts=(), held_as=jnp.bfloat16):
    entries = jax.random.normal(key, shape, jnp.float32) * deviation
    if len(cuts) > 0:
        entries = block_scale(key, shape, cuts, -0.22, 0.18) * entries
    return jnp.clip(entries, min=-reach, max=reach).astype(held_as)


def setup_inputs(seed: int = 0) -> dict:
    key_of = jax.random.split(jax.random.key(seed), 9)
    queries = draw_queries(jax.random.fold_in(key_of[8], 71), 0)
    keys = draw_keys(jax.random.fold_in(key_of[8], 71), 0)
    values = normal_values(key_of[2], (CLIPS, SEQ, H * DH), 1.0, 6.0, ((0, 32), (1, 16)))
    grad_out = normal_values(key_of[3], (CLIPS, SEQ, H * DH), 1.0, 6.0, ((0, 32), (1, 16)))
    clip_tokens = draw_clip_tokens(jax.random.fold_in(key_of[8], 71), 0)
    text_tokens = draw_text_tokens(jax.random.fold_in(key_of[8], 71), 0)
    anchor_rank = jax.vmap(lambda own: jax.random.permutation(own, CLIPS))(jax.random.split(key_of[6], CLIPS * N_CTX)).reshape((CLIPS, N_CTX, CLIPS)).astype(jnp.int32)
    send_block = jax.vmap(lambda own: jax.random.permutation(own, CLIPS))(jax.random.split(key_of[7], CLIPS * N_CTX)).reshape((CLIPS, N_CTX, CLIPS)).astype(jnp.int32)
    return {"queries": queries, "keys": keys, "values": values, "grad_out": grad_out, "clip_tokens": clip_tokens, "text_tokens": text_tokens, "anchor_rank": anchor_rank, "send_block": send_block}


def balanced(array, anchor_rank, send_block):
    clip_ids = jnp.arange(CLIPS, dtype=jnp.int32)[:, None, None]
    ctx_ids = jnp.arange(N_CTX, dtype=jnp.int32)[None, :, None]
    source_block = send_block[anchor_rank, ctx_ids, clip_ids].astype(jnp.int32)
    offsets = jnp.arange(MOVE, dtype=jnp.int32)[None, None, None, :]
    source_rows = (ctx_ids[..., None] * TOK_DEV + source_block[..., None] * MOVE + offsets).reshape(CLIPS, SEQ)
    source_ranks = jnp.broadcast_to(anchor_rank[..., None], (CLIPS, N_CTX, CLIPS, MOVE)).reshape(CLIPS, SEQ)
    return array[source_ranks.astype(jnp.int32), source_rows.astype(jnp.int32)]


def live_keys(clip_len, text_len):
    places = jnp.arange(SEQ, dtype=jnp.int32)
    return (places < clip_len) | ((places >= SEQ - TEXT) & (places < SEQ - TEXT + text_len))


def one_head(pieces):
    head_q, head_k, head_v, head_g, alive = pieces
    factor = DH ** -0.5
    scores = jnp.dot(head_q, head_k.T, preferred_element_type=jnp.float32) * factor
    scores = jnp.where(alive[None, :], scores, -jnp.inf)
    row_max = jnp.max(scores, axis=1, keepdims=True)
    expos = jnp.exp(scores - row_max)
    probs = expos / jnp.sum(expos, axis=1, keepdims=True)
    output = jnp.dot(probs.astype(jnp.bfloat16), head_v, preferred_element_type=jnp.float32)
    slopes = jnp.dot(head_g, head_v.T, preferred_element_type=jnp.float32)
    drift = jnp.sum(head_g.astype(jnp.float32) * output, axis=1, keepdims=True)
    mixed = (probs * (slopes - drift)).astype(jnp.bfloat16)
    grads = jnp.dot(mixed, head_k, preferred_element_type=jnp.float32) * factor
    return output.astype(jnp.bfloat16), grads.astype(jnp.bfloat16)


def one_clip(pieces):
    clip_q, clip_k, clip_v, clip_g, clip_len, text_len = pieces
    alive = live_keys(clip_len, text_len)

    def split_heads(array):
        return array.reshape(SEQ, H, DH).transpose(1, 0, 2)

    outputs, grads = lax.map(lambda inner: one_head((inner[0], inner[1], inner[2], inner[3], alive)),
                             (split_heads(clip_q), split_heads(clip_k), split_heads(clip_v), split_heads(clip_g)))
    return outputs.transpose(1, 0, 2).reshape(SEQ, H * DH), grads.transpose(1, 0, 2).reshape(SEQ, H * DH)


def reference(queries, keys, values, grad_out, clip_tokens, text_tokens, anchor_rank, send_block):
    moved_q = balanced(queries, anchor_rank, send_block)
    moved_k = balanced(keys, anchor_rank, send_block)
    moved_v = balanced(values, anchor_rank, send_block)
    moved_g = balanced(grad_out, anchor_rank, send_block)
    attended, query_grad = lax.map(one_clip, (moved_q, moved_k, moved_v, moved_g, clip_tokens, text_tokens))
    return attended, query_grad
```

```python
import functools

import jax
import jax.numpy as jnp
from jax import lax
from jax.experimental import pallas as pl
from jax.experimental.pallas import tpu as pltpu
from jax.sharding import PartitionSpec as P

DH = 128
TEXT = 256
MOVE = 4
PARTS = 4
LOG2E = 1.4426950408889634
MESH = pl.DeviceIdType.MESH


def one_hot(size, source):
    columns = lax.broadcasted_iota(jnp.int32, (source.shape[0], size), 1)
    return (columns == source).astype(jnp.float32).astype(jnp.bfloat16)


def looked_up(table_ref, index, count):
    lanes = lax.broadcasted_iota(jnp.int32, (index.shape[0], count), 1)
    table = jnp.broadcast_to(table_ref[0], (index.shape[0], count))
    return jnp.sum(jnp.where(lanes == index, table, 0), axis=1, keepdims=True)


def kernel(
    ranks, n_ctx, heads,
    clip_ref, text_ref, anchor_ref, send_ref, k_ref, q_ref, v_ref, g_ref,
    out_ref, grad_ref,
    packed, landed, by_head, head_rows, expos, ones_v, output, scale_row, by_head_out, returned,
    send1, recv1, send2, recv2, send3, recv3,
):
    rows = ranks * MOVE
    total = rows * n_ctx
    part_width = heads * DH // PARTS
    part_heads = heads // PARTS
    per_gap = heads // (n_ctx - heads) if n_ctx > heads else heads + n_ctx
    rank = lax.axis_index("dp")
    place = lax.axis_index("ctx")
    factor = DH ** (-0.5)

    def owner_of(head):
        return head + head // per_gap

    my_head = place - place // (per_gap + 1)
    owns = lax.rem(place, per_gap + 1) != per_gap

    barrier = pltpu.get_barrier_semaphore()

    def greet_rank(step, _):
        peer = lax.rem(rank + step, ranks)
        pl.semaphore_signal(barrier, inc=1, device_id=(peer, place), device_id_type=MESH)
        return 0

    def greet_place(step, _):
        peer = lax.rem(place + step, n_ctx)
        pl.semaphore_signal(barrier, inc=1, device_id=(rank, peer), device_id_type=MESH)
        return 0

    lax.fori_loop(1, ranks, greet_rank, 0)
    lax.fori_loop(1, n_ctx, greet_place, 0)

    spread = rows * PARTS
    line = lax.broadcasted_iota(jnp.int32, (spread, 1), 0)
    block = looked_up(send_ref, line // (MOVE * PARTS), ranks)
    to_send = one_hot(spread, lax.rem(line // MOVE, PARTS) * rows + block * MOVE + lax.rem(line, MOVE))
    slot = lax.rem(line, rows)
    origin = looked_up(anchor_ref, slot // MOVE, ranks)
    to_slot = one_hot(spread, origin * (MOVE * PARTS) + (line // rows) * MOVE + lax.rem(line, MOVE))

    def pack(which, ref):
        stacked = jnp.concatenate(
            [ref[0, :, part * part_width:(part + 1) * part_width] for part in range(PARTS)], axis=0
        )
        moved = jnp.dot(to_send, stacked, preferred_element_type=jnp.float32).astype(jnp.bfloat16)
        packed[which] = moved.reshape(ranks, MOVE * PARTS, part_width)

    def send_blocks(which):
        own = pltpu.make_async_copy(packed.at[which, rank], landed.at[which, rank], recv1.at[which])
        own.start()

        def send_to(peer):
            pltpu.make_async_remote_copy(
                src_ref=packed.at[which, peer],
                dst_ref=landed.at[which, rank],
                send_sem=send1.at[which],
                recv_sem=recv1.at[which],
                device_id=(peer, place),
                device_id_type=MESH,
            ).start()

        def both_ways(step, _):
            send_to(lax.rem(rank + step, ranks))
            send_to(lax.rem(rank + ranks - step, ranks))
            return 0

        lax.fori_loop(1, ranks // 2, both_ways, 0)
        send_to(lax.rem(rank + ranks // 2, ranks))

    def scatter_heads(which):
        pltpu.make_async_copy(landed.at[which], landed.at[which], recv1.at[which]).wait()
        arrived = landed[which].reshape(spread, part_width)
        ordered = jnp.dot(to_slot, arrived, preferred_element_type=jnp.float32).astype(jnp.bfloat16)
        for head in range(heads):
            part, column = head // part_heads, head % part_heads
            by_head[which, head] = ordered[part * rows:(part + 1) * rows, column * DH:(column + 1) * DH]

        def send_head(head, _):
            owner = owner_of(head)

            @pl.when(owner == place)
            def _():
                pltpu.make_async_copy(
                    by_head.at[which, head], head_rows.at[which, place], recv2.at[which]
                ).start()

            @pl.when(owner != place)
            def _():
                pltpu.make_async_remote_copy(
                    src_ref=by_head.at[which, head],
                    dst_ref=head_rows.at[which, place],
                    send_sem=send2.at[which],
                    recv_sem=recv2.at[which],
                    device_id=(rank, owner),
                    device_id_type=MESH,
                ).start()

            return 0

        lax.fori_loop(0, heads, send_head, 0)

    def head_arrived(which):
        pltpu.make_async_copy(head_rows.at[which], head_rows.at[which], recv2.at[which]).wait()

    def send_back(which, target, source):
        @pl.when(target == place)
        def _():
            pltpu.make_async_copy(source, returned.at[which, my_head], recv3.at[which]).start()

        @pl.when(target != place)
        def _():
            pltpu.make_async_remote_copy(
                src_ref=source,
                dst_ref=returned.at[which, my_head],
                send_sem=send3.at[which],
                recv_sem=recv3.at[which],
                device_id=(rank, target),
                device_id_type=MESH,
            ).start()

    sources = (k_ref, q_ref, v_ref, g_ref)
    pack(0, sources[0])
    pl.semaphore_wait(barrier, ranks - 1 + n_ctx - 1)
    send_blocks(0)
    for which in range(1, 4):
        pack(which, sources[which])
        send_blocks(which)
    for which in range(4):
        scatter_heads(which)

    @pl.when(owns)
    def _():
        head_arrived(0)
        head_arrived(1)
        head_arrived(2)
        ones_v[:, :DH] = head_rows[2].reshape(total, DH)
        ones_v[:, DH:] = jnp.ones((total, DH), jnp.bfloat16)
        clip_len = clip_ref[rank]
        text_len = text_ref[rank]
        spot = lax.broadcasted_iota(jnp.int32, (1, total), 1)
        alive = (spot < clip_len) | ((spot >= total - TEXT) & (spot < total - TEXT + text_len))
        bias = jnp.where(alive, 0.0, -jnp.inf).astype(jnp.float32)
        last_dims = (((1,), (1,)), ((), ()))

        def forward(step, _):
            tile = lax.rem(place + step, n_ctx)
            scores = lax.dot_general(
                head_rows[1, tile], head_rows[0].reshape(total, DH), last_dims,
                preferred_element_type=jnp.float32,
            ) + bias
            peak = jnp.max(scores, axis=1, keepdims=True)
            expo = jnp.exp2((scores - peak) * (factor * LOG2E)).astype(jnp.bfloat16)
            expos[tile] = expo
            summed = jnp.dot(expo, ones_v[...], preferred_element_type=jnp.float32)
            inverse = 1.0 / summed[:, DH:]
            result = summed[:, :DH] * inverse
            scale_row[tile] = inverse * factor
            output[tile] = result
            by_head_out[0, tile] = result.astype(jnp.bfloat16)
            send_back(0, tile, by_head_out.at[0, tile])
            return 0

        def backward(step, _):
            tile = lax.rem(place + step, n_ctx)
            cotangent = head_rows[3, tile]
            slopes = lax.dot_general(
                cotangent, head_rows[2].reshape(total, DH), last_dims,
                preferred_element_type=jnp.float32,
            )
            drift = jnp.sum(cotangent.astype(jnp.float32) * output[tile], axis=1, keepdims=True)
            mixed = (expos[tile].astype(jnp.float32) * (slopes - drift)).astype(jnp.bfloat16)
            grads = jnp.dot(mixed, head_rows[0].reshape(total, DH), preferred_element_type=jnp.float32)
            by_head_out[1, tile] = (grads * scale_row[tile]).astype(jnp.bfloat16)
            send_back(1, tile, by_head_out.at[1, tile])
            return 0

        lax.fori_loop(0, n_ctx, forward, 0)
        head_arrived(3)
        lax.fori_loop(0, n_ctx, backward, 0)

    for which, ref in ((0, out_ref), (1, grad_ref)):
        pltpu.make_async_copy(returned.at[which], returned.at[which], recv3.at[which]).wait()
        for head in range(heads):
            ref[0, :, head * DH:(head + 1) * DH] = returned[which, head]

    for which in range(4):
        sent = packed.at[which, pl.ds(0, ranks - 1)]
        pltpu.make_async_copy(sent, sent, send1.at[which]).wait()

    @pl.when(owns)
    def _():
        for which in range(4):
            sent = by_head.at[which, pl.ds(0, heads - 1)]
            pltpu.make_async_copy(sent, sent, send2.at[which]).wait()
        for which in range(2):
            sent = by_head_out.at[which, pl.ds(0, n_ctx - 1)]
            pltpu.make_async_copy(sent, sent, send3.at[which]).wait()

    @pl.when(jnp.logical_not(owns))
    def _():
        for which in range(4):
            sent = by_head.at[which]
            pltpu.make_async_copy(sent, sent, send2.at[which]).wait()


def local(ranks, n_ctx, queries, keys, values, grad_out, clip_tokens, text_tokens, anchor_rank, send_block):
    rows, width = queries.shape[1:]
    heads = width // DH
    total = rows * n_ctx
    shape = jax.ShapeDtypeStruct(queries.shape, jnp.bfloat16)
    vmem = pl.BlockSpec(memory_space=pltpu.VMEM)
    smem = pl.BlockSpec(memory_space=pltpu.SMEM)
    part_width = width // PARTS
    return pl.pallas_call(
        functools.partial(kernel, ranks, n_ctx, heads),
        out_shape=(shape, shape),
        in_specs=[smem, smem, vmem, vmem, vmem, vmem, vmem, vmem],
        out_specs=(vmem, vmem),
        scratch_shapes=[
            pltpu.VMEM((4, ranks, MOVE * PARTS, part_width), jnp.bfloat16),
            pltpu.VMEM((4, ranks, MOVE * PARTS, part_width), jnp.bfloat16),
            pltpu.VMEM((4, heads, rows, DH), jnp.bfloat16),
            pltpu.VMEM((4, n_ctx, rows, DH), jnp.bfloat16),
            pltpu.VMEM((n_ctx, rows, total), jnp.bfloat16),
            pltpu.VMEM((total, 2 * DH), jnp.bfloat16),
            pltpu.VMEM((n_ctx, rows, DH), jnp.float32),
            pltpu.VMEM((n_ctx, rows, DH), jnp.float32),
            pltpu.VMEM((2, n_ctx, rows, DH), jnp.bfloat16),
            pltpu.VMEM((2, heads, rows, DH), jnp.bfloat16),
            pltpu.SemaphoreType.DMA((4,)),
            pltpu.SemaphoreType.DMA((4,)),
            pltpu.SemaphoreType.DMA((4,)),
            pltpu.SemaphoreType.DMA((4,)),
            pltpu.SemaphoreType.DMA((2,)),
            pltpu.SemaphoreType.DMA((2,)),
        ],
        compiler_params=pltpu.CompilerParams(
            collective_id=0, has_side_effects=True, vmem_limit_bytes=48 * 1024 * 1024
        ),
        cost_estimate=pl.CostEstimate(
            flops=8 * total * total * DH, bytes_accessed=12 * rows * width, transcendentals=total * total
        ),
    )(clip_tokens, text_tokens, anchor_rank, send_block, keys, queries, values, grad_out)


def solution(mesh):
    split = P("dp", "ctx", None)
    return jax.shard_map(
        functools.partial(local, mesh.shape["dp"], mesh.shape["ctx"]),
        mesh=mesh,
        in_specs=(split, split, split, split, P(), P(), split, split),
        out_specs=(split, split),
        check_vma=False,
    )
```

```python
import functools

import jax
import jax.numpy as jnp
from jax import lax
from jax.experimental import pallas as pl
from jax.experimental.pallas import tpu as pltpu
from jax.sharding import PartitionSpec as P

DH = 128
TEXT = 256
MOVE = 4
PARTS = 4
LOG2E = 1.4426950408889634
MESH = pl.DeviceIdType.MESH
F32 = jnp.float32
BF16 = jnp.bfloat16
LAST_DIMS = (((1,), (1,)), ((), ()))


def one_hot(size, source):
    columns = lax.broadcasted_iota(jnp.int32, (source.shape[0], size), 1)
    return (columns == source).astype(F32).astype(BF16)


def looked_up(table, index):
    count = table.shape[1]
    lanes = lax.broadcasted_iota(jnp.int32, (index.shape[0], count), 1)
    spread = jnp.broadcast_to(table, (index.shape[0], count))
    return jnp.sum(jnp.where(lanes == index, spread, 0), axis=1, keepdims=True)


def moved_rows(order, array):
    return jnp.dot(order, array, preferred_element_type=F32).astype(BF16)


def all_bytes(ref, sem):
    pltpu.make_async_copy(ref, ref, sem).wait()


def owner_of(head):
    inner = lax.rem(head, 6)
    return head // 6 * 8 + inner + jnp.where(inner >= 3, 1, 0) + jnp.where(inner >= 5, 1, 0)


def head_at(place):
    inner = lax.rem(place, 8)
    head = place // 8 * 6 + inner - jnp.where(inner > 3, 1, 0) - jnp.where(inner > 6, 1, 0)
    return head, (inner != 3) & (inner != 6)


def kernel(
    ranks, n_ctx, heads,
    clip_hbm, text_hbm, anchor_hbm, send_hbm, k_hbm, q_hbm, v_hbm, g_hbm,
    out_ref, grad_ref,
    clip_ref, text_ref, anchor_ref, send_ref, loaded,
    packed, landed, by_head, head_rows,
    columns, column_rows, to_ranks, from_ranks, query_rows,
    expos, ones_v, output, scale_row, results, returned,
    load_sem, dp_send, dp_recv, ctx_send, ctx_recv, back_send, back_recv,
):
    rows = ranks * MOVE
    total = rows * n_ctx
    part_width = heads * DH // PARTS
    part_heads = heads // PARTS
    groups = n_ctx // PARTS
    spread = rows * PARTS
    block_rows = MOVE * PARTS
    rank = lax.axis_index("dp")
    place = lax.axis_index("ctx")
    my_head, owns = head_at(place)
    factor = DH ** (-0.5)

    loads = [
        pltpu.make_async_copy(source, target, load_sem.at[index])
        for index, (source, target) in enumerate((
            (send_hbm, send_ref), (anchor_hbm, anchor_ref),
            (k_hbm, loaded.at[0]), (q_hbm, loaded.at[1]), (v_hbm, loaded.at[2]), (g_hbm, loaded.at[3]),
            (clip_hbm, clip_ref), (text_hbm, text_ref),
        ))
    ]
    for load in loads:
        load.start()

    barrier = pltpu.get_barrier_semaphore()

    def greet_rank(step, _):
        peer = lax.rem(rank + step, ranks)
        pl.semaphore_signal(barrier, inc=1, device_id=(peer, place), device_id_type=MESH)
        return 0

    def greet_place(step, _):
        peer = lax.rem(place + step, n_ctx)
        pl.semaphore_signal(barrier, inc=1, device_id=(rank, peer), device_id_type=MESH)
        return 0

    lax.fori_loop(1, ranks, greet_rank, 0)
    lax.fori_loop(1, n_ctx, greet_place, 0)

    loads[0].wait()
    loads[1].wait()
    line = lax.broadcasted_iota(jnp.int32, (spread, 1), 0)
    short = lax.broadcasted_iota(jnp.int32, (rows, 1), 0)
    inner = lax.rem(line, MOVE)
    send_table, anchor_table = send_ref[0], anchor_ref[0]
    block = looked_up(send_table, line // block_rows)
    to_send = one_hot(spread, lax.rem(line // MOVE, PARTS) * rows + block * MOVE + inner)
    origin = looked_up(anchor_table, lax.rem(line, rows) // MOVE)
    to_slot = one_hot(spread, origin * block_rows + (line // rows) * MOVE + inner)
    to_clip = one_hot(rows, looked_up(send_table, short // MOVE) * MOVE + lax.rem(short, MOVE))
    mix = one_hot(spread, lax.rem(line // MOVE, PARTS) * rows + (line // block_rows) * MOVE + inner)
    unmix = one_hot(spread, (lax.rem(line, rows) // MOVE) * block_rows + (line // rows) * MOVE + inner)
    to_output = one_hot(rows, looked_up(anchor_table, short // MOVE) * MOVE + lax.rem(short, MOVE))

    def pack_blocks(which, array):
        stacked = jnp.concatenate(
            [array[:, part * part_width:(part + 1) * part_width] for part in range(PARTS)], axis=0
        )
        packed[which] = moved_rows(to_send, stacked).reshape(ranks, block_rows, part_width)

    def pack_columns(which, array):
        ordered = moved_rows(to_clip, array)
        for head in range(heads):
            columns[which, head] = ordered[:, head * DH:(head + 1) * DH]

    def over_ranks(source, target, which):
        pltpu.make_async_copy(source.at[rank], target.at[rank], dp_recv.at[which]).start()

        def send_to(peer):
            pltpu.make_async_remote_copy(
                src_ref=source.at[peer],
                dst_ref=target.at[rank],
                send_sem=dp_send.at[which],
                recv_sem=dp_recv.at[which],
                device_id=(peer, place),
                device_id_type=MESH,
            ).start()

        def both_ways(step, _):
            send_to(lax.rem(rank + step, ranks))
            send_to(lax.rem(rank + ranks - step, ranks))
            return 0

        lax.fori_loop(1, ranks // 2, both_ways, 0)
        send_to(lax.rem(rank + ranks // 2, ranks))

    def over_heads(source, target, which):
        def send_head(step, _):
            head = lax.rem(step + place, heads)
            owner = owner_of(head)

            @pl.when(owner == place)
            def _():
                pltpu.make_async_copy(source.at[head], target.at[place], ctx_recv.at[which]).start()

            @pl.when(owner != place)
            def _():
                pltpu.make_async_remote_copy(
                    src_ref=source.at[head],
                    dst_ref=target.at[place],
                    send_sem=ctx_send.at[which],
                    recv_sem=ctx_recv.at[which],
                    device_id=(rank, owner),
                    device_id_type=MESH,
                ).start()

            return 0

        lax.fori_loop(0, heads, send_head, 0)

    def to_place(which, target):
        source = results.at[which, target]

        @pl.when(target == place)
        def _():
            pltpu.make_async_copy(source, returned.at[which, my_head], back_recv.at[which]).start()

        @pl.when(target != place)
        def _():
            pltpu.make_async_remote_copy(
                src_ref=source,
                dst_ref=returned.at[which, my_head],
                send_sem=back_send.at[which],
                recv_sem=back_recv.at[which],
                device_id=(rank, target),
                device_id_type=MESH,
            ).start()

    def scatter_blocks(which):
        all_bytes(landed.at[which], dp_recv.at[which])
        ordered = moved_rows(to_slot, landed[which].reshape(spread, part_width))
        for head in range(heads):
            part, column = head // part_heads, head % part_heads
            by_head[which, head] = ordered[part * rows:(part + 1) * rows, column * DH:(column + 1) * DH]
        over_heads(by_head.at[which], head_rows.at[which], which)

    def scatter_columns(which):
        all_bytes(column_rows.at[which], ctx_recv.at[2 + which])
        gathered = jnp.concatenate(
            [
                column_rows[which, group * PARTS:(group + 1) * PARTS].reshape(spread, DH)
                for group in range(groups)
            ],
            axis=1,
        )
        mixed = moved_rows(mix, gathered)
        for group in range(groups):
            piece = mixed[:, group * DH:(group + 1) * DH]
            to_ranks[which, :, group] = piece.reshape(ranks, block_rows, DH)
        over_ranks(to_ranks.at[which], from_ranks.at[which], 2 + which)

    def take_columns(which):
        all_bytes(from_ranks.at[which], dp_recv.at[2 + which])
        gathered = jnp.concatenate(
            [from_ranks[which, :, group].reshape(spread, DH) for group in range(groups)], axis=1
        )
        unmixed = moved_rows(unmix, gathered)
        for group in range(groups):
            query_rows[which, group] = unmixed[:, group * DH:(group + 1) * DH]

    loads[2].wait()
    pack_blocks(0, loaded[0, 0])
    pl.semaphore_wait(barrier, ranks - 1 + n_ctx - 1)
    over_ranks(packed.at[0], landed.at[0], 0)
    loads[3].wait()
    pack_columns(0, loaded[1, 0])
    over_heads(columns.at[0], column_rows.at[0], 2)
    loads[4].wait()
    pack_blocks(1, loaded[2, 0])
    over_ranks(packed.at[1], landed.at[1], 1)
    loads[5].wait()
    pack_columns(1, loaded[3, 0])
    over_heads(columns.at[1], column_rows.at[1], 3)
    loads[6].wait()
    loads[7].wait()

    scatter_blocks(0)

    @pl.when(owns)
    def _():
        scatter_columns(0)

    scatter_blocks(1)

    @pl.when(owns)
    def _():
        scatter_columns(1)
        all_bytes(head_rows.at[0], ctx_recv.at[0])
        take_columns(0)
        clip_len = clip_ref[rank]
        text_len = text_ref[rank]
        spot = lax.broadcasted_iota(jnp.int32, (1, total), 1)
        alive = (spot < clip_len) | ((spot >= total - TEXT) & (spot < total - TEXT + text_len))
        bias = jnp.where(alive, 0.0, -jnp.inf).astype(F32)

        def weigh(group, _):
            scores = lax.dot_general(
                query_rows[0, group], head_rows[0].reshape(total, DH), LAST_DIMS, preferred_element_type=F32
            ) + bias
            peak = jnp.max(scores, axis=1, keepdims=True)
            expos[group] = jnp.exp2((scores - peak) * (factor * LOG2E)).astype(BF16)
            return 0

        def forward(step, _):
            group = lax.rem(place // PARTS + step, groups)
            summed = jnp.dot(expos[group], ones_v[...], preferred_element_type=F32)
            inverse = 1.0 / summed[:, DH:]
            result = summed[:, :DH] * inverse
            scale_row[group] = inverse * factor
            output[group] = result
            results[0, pl.ds(group * PARTS, PARTS)] = result.astype(BF16).reshape(PARTS, rows, DH)
            for part in range(PARTS):
                to_place(0, group * PARTS + part)
            return 0

        def backward(step, _):
            group = lax.rem(place // PARTS + step, groups)
            cotangent = query_rows[1, group]
            slopes = lax.dot_general(
                cotangent, head_rows[1].reshape(total, DH), LAST_DIMS, preferred_element_type=F32
            )
            drift = jnp.sum(cotangent.astype(F32) * output[group], axis=1, keepdims=True)
            mixed = (expos[group].astype(F32) * (slopes - drift)).astype(BF16)
            grads = jnp.dot(mixed, head_rows[0].reshape(total, DH), preferred_element_type=F32)
            result = (grads * scale_row[group]).astype(BF16)
            results[1, pl.ds(group * PARTS, PARTS)] = result.reshape(PARTS, rows, DH)
            for part in range(PARTS):
                to_place(1, group * PARTS + part)
            return 0

        lax.fori_loop(0, groups, weigh, 0)
        all_bytes(head_rows.at[1], ctx_recv.at[1])
        ones_v[:, :DH] = head_rows[1].reshape(total, DH)
        ones_v[:, DH:] = jnp.ones((total, DH), BF16)
        lax.fori_loop(0, groups, forward, 0)
        take_columns(1)
        lax.fori_loop(0, groups, backward, 0)

    for which, ref in ((0, out_ref), (1, grad_ref)):
        all_bytes(returned.at[which], back_recv.at[which])
        together = jnp.concatenate([returned[which, head] for head in range(heads)], axis=1)
        ref[0] = moved_rows(to_output, together)

    for which in range(2):
        all_bytes(packed.at[which, pl.ds(0, ranks - 1)], dp_send.at[which])

    @pl.when(owns)
    def _():
        for which in range(2):
            all_bytes(by_head.at[which, pl.ds(0, heads - 1)], ctx_send.at[which])
            all_bytes(columns.at[which, pl.ds(0, heads - 1)], ctx_send.at[2 + which])
            all_bytes(to_ranks.at[which, pl.ds(0, ranks - 1)], dp_send.at[2 + which])
            all_bytes(results.at[which, pl.ds(0, n_ctx - 1)], back_send.at[which])

    @pl.when(jnp.logical_not(owns))
    def _():
        for which in range(2):
            all_bytes(by_head.at[which], ctx_send.at[which])
            all_bytes(columns.at[which], ctx_send.at[2 + which])


def local(ranks, n_ctx, queries, keys, values, grad_out, clip_tokens, text_tokens, anchor_rank, send_block):
    rows, width = queries.shape[1:]
    heads = width // DH
    total = rows * n_ctx
    groups = n_ctx // PARTS
    block_rows = MOVE * PARTS
    spread = rows * PARTS
    shape = jax.ShapeDtypeStruct(queries.shape, BF16)
    anywhere = pl.BlockSpec(memory_space=pl.ANY)
    vmem = pl.BlockSpec(memory_space=pltpu.VMEM)
    blocks = pltpu.VMEM((2, ranks, block_rows, width // PARTS), BF16)
    head_blocks = pltpu.VMEM((2, heads, rows, DH), BF16)
    place_blocks = pltpu.VMEM((2, n_ctx, rows, DH), BF16)
    rank_blocks = pltpu.VMEM((2, ranks, groups, block_rows, DH), BF16)
    return pl.pallas_call(
        functools.partial(kernel, ranks, n_ctx, heads),
        out_shape=(shape, shape),
        in_specs=[anywhere] * 8,
        out_specs=(vmem, vmem),
        scratch_shapes=[
            pltpu.SMEM(clip_tokens.shape, jnp.int32),
            pltpu.SMEM(text_tokens.shape, jnp.int32),
            pltpu.VMEM(anchor_rank.shape, jnp.int32),
            pltpu.VMEM(send_block.shape, jnp.int32),
            pltpu.VMEM((4,) + queries.shape, BF16),
            blocks,
            blocks,
            head_blocks,
            place_blocks,
            head_blocks,
            place_blocks,
            rank_blocks,
            rank_blocks,
            pltpu.VMEM((2, groups, spread, DH), BF16),
            pltpu.VMEM((groups, spread, total), BF16),
            pltpu.VMEM((total, 2 * DH), BF16),
            pltpu.VMEM((groups, spread, DH), F32),
            pltpu.VMEM((groups, spread, DH), F32),
            place_blocks,
            head_blocks,
            pltpu.SemaphoreType.DMA((8,)),
            pltpu.SemaphoreType.DMA((4,)),
            pltpu.SemaphoreType.DMA((4,)),
            pltpu.SemaphoreType.DMA((4,)),
            pltpu.SemaphoreType.DMA((4,)),
            pltpu.SemaphoreType.DMA((2,)),
            pltpu.SemaphoreType.DMA((2,)),
        ],
        compiler_params=pltpu.CompilerParams(
            collective_id=0, has_side_effects=True, vmem_limit_bytes=56 * 1024 * 1024
        ),
        cost_estimate=pl.CostEstimate(
            flops=8 * total * total * DH, bytes_accessed=12 * rows * width, transcendentals=total * total
        ),
    )(clip_tokens, text_tokens, anchor_rank, send_block, keys, queries, values, grad_out)


def solution(mesh):
    split = P("dp", "ctx", None)
    return jax.shard_map(
        functools.partial(local, mesh.shape["dp"], mesh.shape["ctx"]),
        mesh=mesh,
        in_specs=(split, split, split, split, P(), P(), split, split),
        out_specs=(split, split),
        check_vma=False,
    )
```

```python
import functools

import jax
import jax.numpy as jnp
from jax import lax
from jax.experimental import pallas as pl
from jax.experimental.pallas import tpu as pltpu
from jax.sharding import PartitionSpec as P

DH = 128
TEXT = 256
MOVE = 4
PARTS = 4
LOG2E = 1.4426950408889634
KINDS = 4
MESH = pl.DeviceIdType.MESH
F32 = jnp.float32
BF16 = jnp.bfloat16
LAST_DIMS = (((1,), (1,)), ((), ()))


def one_hot(size, source):
    columns = lax.broadcasted_iota(jnp.int32, (source.shape[0], size), 1)
    return (columns == source).astype(F32).astype(BF16)


def looked_up(table, index):
    count = table.shape[1]
    lanes = lax.broadcasted_iota(jnp.int32, (index.shape[0], count), 1)
    spread = jnp.broadcast_to(table, (index.shape[0], count))
    return jnp.sum(jnp.where(lanes == index, spread, 0), axis=1, keepdims=True)


def moved_rows(order, array):
    return jnp.dot(order, array, preferred_element_type=F32).astype(BF16)


def all_bytes(ref, sem):
    pltpu.make_async_copy(ref, ref, sem).wait()


def idle_places(kind):
    plane = 1 - kind // 2
    core = lax.rem(kind, 2)
    first = 2 * (plane + 2 * core)
    second = 2 * (plane + 2 * (1 - core)) + 1
    return jnp.minimum(first, second), jnp.maximum(first, second)


def owner_of(kind, head):
    low, high = idle_places(kind)
    inner = lax.rem(head, 6)
    inner = inner + jnp.where(inner >= low, 1, 0)
    inner = inner + jnp.where(inner >= high, 1, 0)
    return head // 6 * 8 + inner


def head_at(kind, place):
    low, high = idle_places(kind)
    inner = lax.rem(place, 8)
    head = place // 8 * 6 + inner - jnp.where(inner > low, 1, 0) - jnp.where(inner > high, 1, 0)
    return head, (inner != low) & (inner != high)


def idle_kind(place):
    plane, side = lax.rem(place // 2, 4), lax.rem(place, 2)
    return (1 - lax.rem(plane, 2)) * 2 + lax.rem(plane // 2 + side, 2)


def kernel(
    ranks, n_ctx, heads,
    clip_hbm, text_hbm, anchor_hbm, send_hbm, k_hbm, q_hbm, v_hbm, g_hbm,
    out_ref, grad_ref,
    clip_ref, text_ref, anchor_ref, send_ref, loaded,
    packed, landed, by_head, head_rows,
    columns, column_rows, to_ranks, from_ranks, query_rows,
    expos, ones_v, output, scale_row, results, returned,
    load_sem, dp_send, dp_recv, ctx_send, ctx_recv, back_send, back_recv,
):
    rows = ranks * MOVE
    total = rows * n_ctx
    part_width = heads * DH // PARTS
    part_heads = heads // PARTS
    groups = n_ctx // PARTS
    spread = rows * PARTS
    block_rows = MOVE * PARTS
    rank = lax.axis_index("dp")
    place = lax.axis_index("ctx")
    kind = lax.rem(rank, KINDS)
    my_head, owns = head_at(kind, place)
    idle = idle_kind(place)
    per_kind = ranks // KINDS
    kind_rows = rows // KINDS
    factor = DH ** (-0.5)

    loads = [
        pltpu.make_async_copy(source, target, load_sem.at[index])
        for index, (source, target) in enumerate((
            (send_hbm, send_ref), (anchor_hbm, anchor_ref),
            (k_hbm, loaded.at[0]), (q_hbm, loaded.at[1]), (v_hbm, loaded.at[2]), (g_hbm, loaded.at[3]),
            (clip_hbm, clip_ref), (text_hbm, text_ref),
        ))
    ]
    for load in loads:
        load.start()

    for which in range(2):
        column_rows[which, :, pl.ds(pl.multiple_of(idle * kind_rows, kind_rows), kind_rows)] = jnp.zeros(
            (n_ctx, kind_rows, DH), BF16
        )

    barrier = pltpu.get_barrier_semaphore()

    def greet_rank(step, _):
        peer = lax.rem(rank + step, ranks)
        pl.semaphore_signal(barrier, inc=1, device_id=(peer, place), device_id_type=MESH)
        return 0

    def greet_place(step, _):
        peer = lax.rem(place + step, n_ctx)
        pl.semaphore_signal(barrier, inc=1, device_id=(rank, peer), device_id_type=MESH)
        return 0

    lax.fori_loop(1, ranks, greet_rank, 0)
    lax.fori_loop(1, n_ctx, greet_place, 0)

    loads[0].wait()
    loads[1].wait()
    line = lax.broadcasted_iota(jnp.int32, (spread, 1), 0)
    short = lax.broadcasted_iota(jnp.int32, (rows, 1), 0)
    inner = lax.rem(line, MOVE)
    send_table, anchor_table = send_ref[0], anchor_ref[0]
    block = looked_up(send_table, line // block_rows)
    to_send = one_hot(spread, lax.rem(line // MOVE, PARTS) * rows + block * MOVE + inner)
    origin = looked_up(anchor_table, lax.rem(line, rows) // MOVE)
    to_slot = one_hot(spread, origin * block_rows + (line // rows) * MOVE + inner)
    clip = lax.rem(short // MOVE, per_kind) * KINDS + short // kind_rows
    to_clip = one_hot(rows, looked_up(send_table, clip) * MOVE + lax.rem(short, MOVE))
    mix = one_hot(spread, lax.rem(line // MOVE, PARTS) * rows + (line // block_rows) * MOVE + inner)
    unmix = one_hot(spread, (lax.rem(line, rows) // MOVE) * block_rows + (line // rows) * MOVE + inner)
    to_output = one_hot(rows, looked_up(anchor_table, short // MOVE) * MOVE + lax.rem(short, MOVE))

    def pack_blocks(which, array):
        stacked = jnp.concatenate(
            [array[:, part * part_width:(part + 1) * part_width] for part in range(PARTS)], axis=0
        )
        packed[which] = moved_rows(to_send, stacked).reshape(ranks, block_rows, part_width)

    def pack_columns(which, array):
        ordered = moved_rows(to_clip, array)
        for head in range(heads):
            columns[which, head] = ordered[:, head * DH:(head + 1) * DH]

    def over_ranks(source, target, which):
        pltpu.make_async_copy(source.at[rank], target.at[rank], dp_recv.at[which]).start()

        def send_to(peer):
            pltpu.make_async_remote_copy(
                src_ref=source.at[peer],
                dst_ref=target.at[rank],
                send_sem=dp_send.at[which],
                recv_sem=dp_recv.at[which],
                device_id=(peer, place),
                device_id_type=MESH,
            ).start()

        def both_ways(step, _):
            send_to(lax.rem(rank + step, ranks))
            send_to(lax.rem(rank + ranks - step, ranks))
            return 0

        lax.fori_loop(1, ranks // 2, both_ways, 0)
        send_to(lax.rem(rank + ranks // 2, ranks))

    def over_heads(source, target, which):
        def send_head(step, _):
            head = lax.rem(step + place, heads)
            owner = owner_of(kind, head)

            @pl.when(owner == place)
            def _():
                pltpu.make_async_copy(source.at[head], target.at[place], ctx_recv.at[which]).start()

            @pl.when(owner != place)
            def _():
                pltpu.make_async_remote_copy(
                    src_ref=source.at[head],
                    dst_ref=target.at[place],
                    send_sem=ctx_send.at[which],
                    recv_sem=ctx_recv.at[which],
                    device_id=(rank, owner),
                    device_id_type=MESH,
                ).start()

            return 0

        lax.fori_loop(0, heads, send_head, 0)

    def columns_to_owners(which):
        def send_head(step, _):
            head = lax.rem(step + place, heads)
            for target_kind in range(KINDS):
                owner = owner_of(target_kind, head)
                part = pl.ds(target_kind * kind_rows, kind_rows)
                source = columns.at[which, head, part]
                target = column_rows.at[which, place, part]

                @pl.when(owner == place)
                def _(source=source, target=target):
                    pltpu.make_async_copy(source, target, ctx_recv.at[2 + which]).start()

                @pl.when(owner != place)
                def _(source=source, target=target, owner=owner):
                    pltpu.make_async_remote_copy(
                        src_ref=source,
                        dst_ref=target,
                        send_sem=ctx_send.at[2 + which],
                        recv_sem=ctx_recv.at[2 + which],
                        device_id=(rank, owner),
                        device_id_type=MESH,
                    ).start()

            return 0

        lax.fori_loop(0, heads, send_head, 0)

    def columns_to_ranks(which):
        def send_row(step, _):
            offset = jnp.where(lax.rem(step, 2) == 1, (step + 1) // 2, per_kind - step // 2)
            row = lax.rem(rank // KINDS + offset, per_kind)
            for target_kind in range(KINDS):
                peer = row * KINDS + target_kind
                source = to_ranks.at[which, target_kind * per_kind + row]
                target = from_ranks.at[which, rank]

                @pl.when((target_kind != idle) & (peer == rank))
                def _(source=source, target=target):
                    pltpu.make_async_copy(source, target, dp_recv.at[2 + which]).start()

                @pl.when((target_kind != idle) & (peer != rank))
                def _(source=source, target=target, peer=peer):
                    pltpu.make_async_remote_copy(
                        src_ref=source,
                        dst_ref=target,
                        send_sem=dp_send.at[2 + which],
                        recv_sem=dp_recv.at[2 + which],
                        device_id=(peer, place),
                        device_id_type=MESH,
                    ).start()

            return 0

        lax.fori_loop(0, per_kind, send_row, 0)

    def to_place(which, target):
        source = results.at[which, target]

        @pl.when(target == place)
        def _():
            pltpu.make_async_copy(source, returned.at[which, my_head], back_recv.at[which]).start()

        @pl.when(target != place)
        def _():
            pltpu.make_async_remote_copy(
                src_ref=source,
                dst_ref=returned.at[which, my_head],
                send_sem=back_send.at[which],
                recv_sem=back_recv.at[which],
                device_id=(rank, target),
                device_id_type=MESH,
            ).start()

    def scatter_blocks(which):
        all_bytes(landed.at[which], dp_recv.at[which])
        ordered = moved_rows(to_slot, landed[which].reshape(spread, part_width))
        for head in range(heads):
            part, column = head // part_heads, head % part_heads
            by_head[which, head] = ordered[part * rows:(part + 1) * rows, column * DH:(column + 1) * DH]
        over_heads(by_head.at[which], head_rows.at[which], which)

    def scatter_columns(which):
        all_bytes(column_rows.at[which, pl.ds(0, n_ctx // KINDS * (KINDS - 1))], ctx_recv.at[2 + which])
        gathered = jnp.concatenate(
            [
                column_rows[which, group * PARTS:(group + 1) * PARTS].reshape(spread, DH)
                for group in range(groups)
            ],
            axis=1,
        )
        mixed = moved_rows(mix, gathered)
        for group in range(groups):
            piece = mixed[:, group * DH:(group + 1) * DH]
            to_ranks[which, :, group] = piece.reshape(ranks, block_rows, DH)
        columns_to_ranks(which)

    def take_columns(which):
        all_bytes(from_ranks.at[which], dp_recv.at[2 + which])
        gathered = jnp.concatenate(
            [from_ranks[which, :, group].reshape(spread, DH) for group in range(groups)], axis=1
        )
        unmixed = moved_rows(unmix, gathered)
        for group in range(groups):
            query_rows[which, group] = unmixed[:, group * DH:(group + 1) * DH]

    loads[2].wait()
    pack_blocks(0, loaded[0, 0])
    pl.semaphore_wait(barrier, ranks - 1 + n_ctx - 1)
    over_ranks(packed.at[0], landed.at[0], 0)
    loads[3].wait()
    pack_columns(0, loaded[1, 0])
    columns_to_owners(0)
    loads[4].wait()
    pack_blocks(1, loaded[2, 0])
    over_ranks(packed.at[1], landed.at[1], 1)
    loads[5].wait()
    pack_columns(1, loaded[3, 0])
    columns_to_owners(1)
    loads[6].wait()
    loads[7].wait()

    scatter_blocks(0)
    scatter_columns(0)
    scatter_blocks(1)
    scatter_columns(1)

    @pl.when(owns)
    def _():
        all_bytes(head_rows.at[0], ctx_recv.at[0])
        take_columns(0)
        clip_len = clip_ref[rank]
        text_len = text_ref[rank]
        spot = lax.broadcasted_iota(jnp.int32, (1, total), 1)
        alive = (spot < clip_len) | ((spot >= total - TEXT) & (spot < total - TEXT + text_len))
        bias = jnp.where(alive, 0.0, -jnp.inf).astype(F32)

        def weigh(group, _):
            scores = lax.dot_general(
                query_rows[0, group], head_rows[0].reshape(total, DH), LAST_DIMS, preferred_element_type=F32
            ) + bias
            peak = jnp.max(scores, axis=1, keepdims=True)
            expos[group] = jnp.exp2((scores - peak) * (factor * LOG2E)).astype(BF16)
            return 0

        def forward(step, _):
            group = lax.rem(place // PARTS + step, groups)
            summed = jnp.dot(expos[group], ones_v[...], preferred_element_type=F32)
            inverse = 1.0 / summed[:, DH:]
            result = summed[:, :DH] * inverse
            scale_row[group] = inverse * factor
            output[group] = result
            results[0, pl.ds(group * PARTS, PARTS)] = result.astype(BF16).reshape(PARTS, rows, DH)
            for part in range(PARTS):
                to_place(0, group * PARTS + part)
            return 0

        def backward(step, _):
            group = lax.rem(place // PARTS + step, groups)
            cotangent = query_rows[1, group]
            slopes = lax.dot_general(
                cotangent, head_rows[1].reshape(total, DH), LAST_DIMS, preferred_element_type=F32
            )
            drift = jnp.sum(cotangent.astype(F32) * output[group], axis=1, keepdims=True)
            mixed = (expos[group].astype(F32) * (slopes - drift)).astype(BF16)
            grads = jnp.dot(mixed, head_rows[0].reshape(total, DH), preferred_element_type=F32)
            result = (grads * scale_row[group]).astype(BF16)
            results[1, pl.ds(group * PARTS, PARTS)] = result.reshape(PARTS, rows, DH)
            for part in range(PARTS):
                to_place(1, group * PARTS + part)
            return 0

        lax.fori_loop(0, groups, weigh, 0)
        all_bytes(head_rows.at[1], ctx_recv.at[1])
        ones_v[:, :DH] = head_rows[1].reshape(total, DH)
        ones_v[:, DH:] = jnp.ones((total, DH), BF16)
        lax.fori_loop(0, groups, forward, 0)
        take_columns(1)
        lax.fori_loop(0, groups, backward, 0)

    for which, ref in ((0, out_ref), (1, grad_ref)):
        all_bytes(returned.at[which], back_recv.at[which])
        together = jnp.concatenate([returned[which, head] for head in range(heads)], axis=1)
        ref[0] = moved_rows(to_output, together)

    for which in range(2):
        all_bytes(packed.at[which, pl.ds(0, ranks - 1)], dp_send.at[which])
        all_bytes(columns.at[which, pl.ds(0, heads - 1)], ctx_send.at[2 + which])
        all_bytes(columns.at[which, 0, pl.ds(0, kind_rows)], ctx_send.at[2 + which])

    @pl.when(owns)
    def _():
        for which in range(2):
            all_bytes(by_head.at[which, pl.ds(0, heads - 1)], ctx_send.at[which])
            all_bytes(to_ranks.at[which, pl.ds(0, (KINDS - 1) * per_kind - 1)], dp_send.at[2 + which])
            all_bytes(results.at[which, pl.ds(0, n_ctx - 1)], back_send.at[which])

    @pl.when(jnp.logical_not(owns))
    def _():
        for which in range(2):
            all_bytes(by_head.at[which], ctx_send.at[which])
            all_bytes(to_ranks.at[which, pl.ds(0, (KINDS - 1) * per_kind)], dp_send.at[2 + which])


def local(ranks, n_ctx, queries, keys, values, grad_out, clip_tokens, text_tokens, anchor_rank, send_block):
    rows, width = queries.shape[1:]
    heads = width // DH
    total = rows * n_ctx
    groups = n_ctx // PARTS
    block_rows = MOVE * PARTS
    spread = rows * PARTS
    shape = jax.ShapeDtypeStruct(queries.shape, BF16)
    anywhere = pl.BlockSpec(memory_space=pl.ANY)
    vmem = pl.BlockSpec(memory_space=pltpu.VMEM)
    blocks = pltpu.VMEM((2, ranks, block_rows, width // PARTS), BF16)
    head_blocks = pltpu.VMEM((2, heads, rows, DH), BF16)
    place_blocks = pltpu.VMEM((2, n_ctx, rows, DH), BF16)
    rank_blocks = pltpu.VMEM((2, ranks, groups, block_rows, DH), BF16)
    return pl.pallas_call(
        functools.partial(kernel, ranks, n_ctx, heads),
        out_shape=(shape, shape),
        in_specs=[anywhere] * 8,
        out_specs=(vmem, vmem),
        scratch_shapes=[
            pltpu.SMEM(clip_tokens.shape, jnp.int32),
            pltpu.SMEM(text_tokens.shape, jnp.int32),
            pltpu.VMEM(anchor_rank.shape, jnp.int32),
            pltpu.VMEM(send_block.shape, jnp.int32),
            pltpu.VMEM((4,) + queries.shape, BF16),
            blocks,
            blocks,
            head_blocks,
            place_blocks,
            head_blocks,
            place_blocks,
            rank_blocks,
            rank_blocks,
            pltpu.VMEM((2, groups, spread, DH), BF16),
            pltpu.VMEM((groups, spread, total), BF16),
            pltpu.VMEM((total, 2 * DH), BF16),
            pltpu.VMEM((groups, spread, DH), F32),
            pltpu.VMEM((groups, spread, DH), F32),
            place_blocks,
            head_blocks,
            pltpu.SemaphoreType.DMA((8,)),
            pltpu.SemaphoreType.DMA((4,)),
            pltpu.SemaphoreType.DMA((4,)),
            pltpu.SemaphoreType.DMA((4,)),
            pltpu.SemaphoreType.DMA((4,)),
            pltpu.SemaphoreType.DMA((2,)),
            pltpu.SemaphoreType.DMA((2,)),
        ],
        compiler_params=pltpu.CompilerParams(
            collective_id=0, has_side_effects=True, vmem_limit_bytes=58 * 1024 * 1024
        ),
        cost_estimate=pl.CostEstimate(
            flops=8 * total * total * DH, bytes_accessed=12 * rows * width, transcendentals=total * total
        ),
    )(clip_tokens, text_tokens, anchor_rank, send_block, keys, queries, values, grad_out)


def solution(mesh):
    split = P("dp", "ctx", None)
    return jax.shard_map(
        functools.partial(local, mesh.shape["dp"], mesh.shape["ctx"]),
        mesh=mesh,
        in_specs=(split, split, split, split, P(), P(), split, split),
        out_specs=(split, split),
        check_vma=False,
    )
```

```python
import functools

import jax
import jax.numpy as jnp
from jax import lax
from jax.experimental import pallas as pl
from jax.experimental.pallas import tpu as pltpu
from jax.sharding import PartitionSpec as P

DH = 128
TEXT = 256
MOVE = 4
PARTS = 4
LOG2E = 1.4426950408889634
KINDS = 4
MESH = pl.DeviceIdType.MESH
F32 = jnp.float32
BF16 = jnp.bfloat16
LAST_DIMS = (((1,), (1,)), ((), ()))


def one_hot(size, source):
    columns = lax.broadcasted_iota(jnp.int32, (source.shape[0], size), 1)
    return (columns == source).astype(F32).astype(BF16)


def looked_up(table, index):
    count = table.shape[1]
    lanes = lax.broadcasted_iota(jnp.int32, (index.shape[0], count), 1)
    spread = jnp.broadcast_to(table, (index.shape[0], count))
    return jnp.sum(jnp.where(lanes == index, spread, 0), axis=1, keepdims=True)


def moved_rows(order, array):
    return jnp.dot(order, array, preferred_element_type=F32).astype(BF16)


def all_bytes(ref, sem):
    pltpu.make_async_copy(ref, ref, sem).wait()


def idle_places(kind):
    plane = 1 - kind // 2
    core = lax.rem(kind, 2)
    first = 2 * (plane + 2 * core)
    second = 2 * (plane + 2 * (1 - core)) + 1
    return jnp.minimum(first, second), jnp.maximum(first, second)


def owner_of(kind, head):
    low, high = idle_places(kind)
    inner = lax.rem(head, 6)
    inner = inner + jnp.where(inner >= low, 1, 0)
    inner = inner + jnp.where(inner >= high, 1, 0)
    return head // 6 * 8 + inner


def head_at(kind, place):
    low, high = idle_places(kind)
    inner = lax.rem(place, 8)
    head = place // 8 * 6 + inner - jnp.where(inner > low, 1, 0) - jnp.where(inner > high, 1, 0)
    return head, (inner != low) & (inner != high)


def idle_kind(place):
    plane, side = lax.rem(place // 2, 4), lax.rem(place, 2)
    return (1 - lax.rem(plane, 2)) * 2 + lax.rem(plane // 2 + side, 2)


def kernel(
    ranks, n_ctx, heads,
    clip_hbm, text_hbm, anchor_hbm, send_hbm, k_hbm, q_hbm, v_hbm, g_hbm,
    returned,
    clip_ref, text_ref, anchor_ref, send_ref, loaded,
    packed, landed, by_head, head_rows,
    columns, column_rows, to_ranks, from_ranks, query_rows,
    expos, ones_v, output, scale_row, results,
    load_sem, dp_send, dp_recv, ctx_send, ctx_recv, back_send, back_recv,
):
    rows = ranks * MOVE
    total = rows * n_ctx
    part_width = heads * DH // PARTS
    part_heads = heads // PARTS
    groups = n_ctx // PARTS
    spread = rows * PARTS
    block_rows = MOVE * PARTS
    rank = lax.axis_index("dp")
    place = lax.axis_index("ctx")
    kind = lax.rem(rank, KINDS)
    my_head, owns = head_at(kind, place)
    idle = idle_kind(place)
    per_kind = ranks // KINDS
    kind_rows = rows // KINDS
    factor = DH ** (-0.5)

    loads = [
        pltpu.make_async_copy(source, target, load_sem.at[index])
        for index, (source, target) in enumerate((
            (send_hbm, send_ref), (anchor_hbm, anchor_ref),
            (k_hbm, loaded.at[0]), (q_hbm, loaded.at[1]), (v_hbm, loaded.at[2]), (g_hbm, loaded.at[3]),
            (clip_hbm, clip_ref), (text_hbm, text_ref),
        ))
    ]
    for load in loads:
        load.start()

    barrier = pltpu.get_barrier_semaphore()

    def greet_rank(step, _):
        peer = lax.rem(rank + step, ranks)
        pl.semaphore_signal(barrier, inc=1, device_id=(peer, place), device_id_type=MESH)
        return 0

    def greet_place(step, _):
        peer = lax.rem(place + step, n_ctx)
        pl.semaphore_signal(barrier, inc=1, device_id=(rank, peer), device_id_type=MESH)
        return 0

    lax.fori_loop(1, ranks, greet_rank, 0)
    lax.fori_loop(1, n_ctx, greet_place, 0)

    loads[0].wait()
    line = lax.broadcasted_iota(jnp.int32, (spread, 1), 0)
    short = lax.broadcasted_iota(jnp.int32, (rows, 1), 0)
    inner = lax.rem(line, MOVE)
    send_table = send_ref[0]
    block = looked_up(send_table, line // block_rows)
    to_send = one_hot(spread, lax.rem(line // MOVE, PARTS) * rows + block * MOVE + inner)
    def pack_blocks(which, array):
        stacked = jnp.concatenate(
            [array[:, part * part_width:(part + 1) * part_width] for part in range(PARTS)], axis=0
        )
        packed[which] = moved_rows(to_send, stacked).reshape(ranks, block_rows, part_width)

    def pack_columns(which, array):
        ordered = moved_rows(to_clip, array)
        for head in range(heads):
            columns[which, head] = ordered[:, head * DH:(head + 1) * DH]

    def far_and_near(step):
        return lax.rem(per_kind // 2 + 3 * step, per_kind)

    def head_in_turn(step):
        return lax.rem(place * heads // n_ctx + 5 * step, heads)

    def over_ranks(source, target, which):
        pltpu.make_async_copy(source.at[rank], target.at[rank], dp_recv.at[which]).start()

        def send_to(peer):
            pltpu.make_async_remote_copy(
                src_ref=source.at[peer],
                dst_ref=target.at[rank],
                send_sem=dp_send.at[which],
                recv_sem=dp_recv.at[which],
                device_id=(peer, place),
                device_id_type=MESH,
            ).start()

        def send_row(step, _):
            row = lax.rem(rank // KINDS + far_and_near(step), per_kind)
            for target_kind in range(KINDS):
                peer = row * KINDS + target_kind

                @pl.when(peer != rank)
                def _(peer=peer):
                    send_to(peer)

            return 0

        lax.fori_loop(0, per_kind, send_row, 0)

    def over_heads(source, target, which):
        def send_head(step, _):
            head = head_in_turn(step)
            owner = owner_of(kind, head)

            @pl.when(owner == place)
            def _():
                pltpu.make_async_copy(source.at[head], target.at[place], ctx_recv.at[which]).start()

            @pl.when(owner != place)
            def _():
                pltpu.make_async_remote_copy(
                    src_ref=source.at[head],
                    dst_ref=target.at[place],
                    send_sem=ctx_send.at[which],
                    recv_sem=ctx_recv.at[which],
                    device_id=(rank, owner),
                    device_id_type=MESH,
                ).start()

            return 0

        lax.fori_loop(0, heads, send_head, 0)

    def columns_to_owners(which):
        def send_head(step, _):
            head = head_in_turn(step)
            for target_kind in range(KINDS):
                owner = owner_of(target_kind, head)
                part = pl.ds(target_kind * kind_rows, kind_rows)
                source = columns.at[which, head, part]
                target = column_rows.at[which, place, part]

                @pl.when(owner == place)
                def _(source=source, target=target):
                    pltpu.make_async_copy(source, target, ctx_recv.at[2 + which]).start()

                @pl.when(owner != place)
                def _(source=source, target=target, owner=owner):
                    pltpu.make_async_remote_copy(
                        src_ref=source,
                        dst_ref=target,
                        send_sem=ctx_send.at[2 + which],
                        recv_sem=ctx_recv.at[2 + which],
                        device_id=(rank, owner),
                        device_id_type=MESH,
                    ).start()

            return 0

        lax.fori_loop(0, heads, send_head, 0)

    def columns_to_ranks(which):
        def send_row(step, _):
            row = lax.rem(rank // KINDS + far_and_near(step), per_kind)
            for target_kind in range(KINDS):
                peer = row * KINDS + target_kind
                source = to_ranks.at[which, target_kind * per_kind + row]
                target = from_ranks.at[which, rank]

                @pl.when((target_kind != idle) & (peer == rank))
                def _(source=source, target=target):
                    pltpu.make_async_copy(source, target, dp_recv.at[2 + which]).start()

                @pl.when((target_kind != idle) & (peer != rank))
                def _(source=source, target=target, peer=peer):
                    pltpu.make_async_remote_copy(
                        src_ref=source,
                        dst_ref=target,
                        send_sem=dp_send.at[2 + which],
                        recv_sem=dp_recv.at[2 + which],
                        device_id=(peer, place),
                        device_id_type=MESH,
                    ).start()

            return 0

        lax.fori_loop(0, per_kind, send_row, 0)

    def to_place(which, target):
        source = results.at[which, target]

        @pl.when(target == place)
        def _():
            pltpu.make_async_copy(source, returned.at[which, my_head], back_recv.at[which]).start()

        @pl.when(target != place)
        def _():
            pltpu.make_async_remote_copy(
                src_ref=source,
                dst_ref=returned.at[which, my_head],
                send_sem=back_send.at[which],
                recv_sem=back_recv.at[which],
                device_id=(rank, target),
                device_id_type=MESH,
            ).start()

    def scatter_blocks(which):
        all_bytes(landed.at[which], dp_recv.at[which])
        ordered = moved_rows(to_slot, landed[which].reshape(spread, part_width))
        for head in range(heads):
            part, column = head // part_heads, head % part_heads
            by_head[which, head] = ordered[part * rows:(part + 1) * rows, column * DH:(column + 1) * DH]
        over_heads(by_head.at[which], head_rows.at[which], which)

    def scatter_columns(which):
        all_bytes(column_rows.at[which, pl.ds(0, n_ctx // KINDS * (KINDS - 1))], ctx_recv.at[2 + which])
        gathered = jnp.concatenate(
            [
                column_rows[which, group * PARTS:(group + 1) * PARTS].reshape(spread, DH)
                for group in range(groups)
            ],
            axis=1,
        )
        mixed = moved_rows(mix, gathered)
        for group in range(groups):
            piece = mixed[:, group * DH:(group + 1) * DH]
            to_ranks[which, :, group] = piece.reshape(ranks, block_rows, DH)
        columns_to_ranks(which)

    def take_columns(which):
        all_bytes(from_ranks.at[which], dp_recv.at[2 + which])
        gathered = jnp.concatenate(
            [from_ranks[which, :, group].reshape(spread, DH) for group in range(groups)], axis=1
        )
        unmixed = moved_rows(unmix, gathered)
        for group in range(groups):
            query_rows[which, group] = unmixed[:, group * DH:(group + 1) * DH]

    loads[2].wait()
    pack_blocks(0, loaded[0, 0])
    pl.semaphore_wait(barrier, ranks - 1 + n_ctx - 1)
    over_ranks(packed.at[0], landed.at[0], 0)
    clip = lax.rem(short // MOVE, per_kind) * KINDS + short // kind_rows
    to_clip = one_hot(rows, looked_up(send_table, clip) * MOVE + lax.rem(short, MOVE))
    loads[3].wait()
    pack_columns(0, loaded[1, 0])
    columns_to_owners(0)
    loads[4].wait()
    pack_blocks(1, loaded[2, 0])
    over_ranks(packed.at[1], landed.at[1], 1)
    loads[5].wait()
    pack_columns(1, loaded[3, 0])
    columns_to_owners(1)
    loads[6].wait()
    loads[7].wait()

    for which in range(2):
        column_rows[which, :, pl.ds(pl.multiple_of(idle * kind_rows, kind_rows), kind_rows)] = jnp.zeros(
            (n_ctx, kind_rows, DH), BF16
        )

    loads[1].wait()
    anchor_table = anchor_ref[0]
    origin = looked_up(anchor_table, lax.rem(line, rows) // MOVE)
    to_slot = one_hot(spread, origin * block_rows + (line // rows) * MOVE + inner)
    mix = one_hot(spread, lax.rem(line // MOVE, PARTS) * rows + (line // block_rows) * MOVE + inner)
    unmix = one_hot(spread, (lax.rem(line, rows) // MOVE) * block_rows + (line // rows) * MOVE + inner)


    scatter_blocks(0)
    scatter_columns(0)
    scatter_blocks(1)
    scatter_columns(1)

    @pl.when(owns)
    def _():
        all_bytes(head_rows.at[0], ctx_recv.at[0])
        take_columns(0)
        clip_len = clip_ref[rank]
        text_len = text_ref[rank]
        spot = lax.broadcasted_iota(jnp.int32, (1, total), 1)
        alive = (spot < clip_len) | ((spot >= total - TEXT) & (spot < total - TEXT + text_len))
        bias = jnp.where(alive, 0.0, -jnp.inf).astype(F32)

        def weigh(group, _):
            scores = lax.dot_general(
                query_rows[0, group], head_rows[0].reshape(total, DH), LAST_DIMS, preferred_element_type=F32
            ) + bias
            peak = jnp.max(scores, axis=1, keepdims=True)
            expos[group] = jnp.exp2((scores - peak) * (factor * LOG2E)).astype(BF16)
            return 0

        def forward(step, _):
            group = lax.rem(place // PARTS + step, groups)
            summed = jnp.dot(expos[group], ones_v[...], preferred_element_type=F32)
            inverse = 1.0 / summed[:, DH:]
            result = summed[:, :DH] * inverse
            scale_row[group] = inverse * factor
            output[group] = result
            results[0, pl.ds(group * PARTS, PARTS)] = result.astype(BF16).reshape(PARTS, rows, DH)
            for part in range(PARTS):
                to_place(0, group * PARTS + part)
            return 0

        def backward(step, _):
            group = lax.rem(place // PARTS + step, groups)
            cotangent = query_rows[1, group]
            slopes = lax.dot_general(
                cotangent, head_rows[1].reshape(total, DH), LAST_DIMS, preferred_element_type=F32
            )
            drift = jnp.sum(cotangent.astype(F32) * output[group], axis=1, keepdims=True)
            mixed = (expos[group].astype(F32) * (slopes - drift)).astype(BF16)
            grads = jnp.dot(mixed, head_rows[0].reshape(total, DH), preferred_element_type=F32)
            result = (grads * scale_row[group]).astype(BF16)
            results[1, pl.ds(group * PARTS, PARTS)] = result.reshape(PARTS, rows, DH)
            for part in range(PARTS):
                to_place(1, group * PARTS + part)
            return 0

        lax.fori_loop(0, groups, weigh, 0)
        all_bytes(head_rows.at[1], ctx_recv.at[1])
        ones_v[:, :DH] = head_rows[1].reshape(total, DH)
        ones_v[:, DH:] = jnp.ones((total, DH), BF16)
        lax.fori_loop(0, groups, forward, 0)
        take_columns(1)
        lax.fori_loop(0, groups, backward, 0)

    for which in range(2):
        all_bytes(returned.at[which], back_recv.at[which])

    for which in range(2):
        all_bytes(packed.at[which, pl.ds(0, ranks - 1)], dp_send.at[which])
        all_bytes(columns.at[which, pl.ds(0, heads - 1)], ctx_send.at[2 + which])
        all_bytes(columns.at[which, 0, pl.ds(0, kind_rows)], ctx_send.at[2 + which])

    @pl.when(owns)
    def _():
        for which in range(2):
            all_bytes(by_head.at[which, pl.ds(0, heads - 1)], ctx_send.at[which])
            all_bytes(to_ranks.at[which, pl.ds(0, (KINDS - 1) * per_kind - 1)], dp_send.at[2 + which])
            all_bytes(results.at[which, pl.ds(0, n_ctx - 1)], back_send.at[which])

    @pl.when(jnp.logical_not(owns))
    def _():
        for which in range(2):
            all_bytes(by_head.at[which], ctx_send.at[which])
            all_bytes(to_ranks.at[which, pl.ds(0, (KINDS - 1) * per_kind)], dp_send.at[2 + which])


def in_slot_order(heads, anchor_hbm, returned_hbm, out_hbm, grad_hbm, anchor_ref, returned, ordered, load_sem, store_sem):
    rows = returned.shape[2]
    loads = [
        pltpu.make_async_copy(anchor_hbm, anchor_ref, load_sem.at[2]),
        pltpu.make_async_copy(returned_hbm.at[0], returned.at[0], load_sem.at[0]),
        pltpu.make_async_copy(returned_hbm.at[1], returned.at[1], load_sem.at[1]),
    ]
    stores = [
        pltpu.make_async_copy(ordered.at[0], out_hbm, store_sem.at[0]),
        pltpu.make_async_copy(ordered.at[1], grad_hbm, store_sem.at[1]),
    ]
    for load in loads:
        load.start()
    loads[0].wait()
    line = lax.broadcasted_iota(jnp.int32, (rows, 1), 0)
    to_output = one_hot(rows, looked_up(anchor_ref[0], line // MOVE) * MOVE + lax.rem(line, MOVE))
    for which in range(2):
        loads[1 + which].wait()
        together = jnp.concatenate([returned[which, head] for head in range(heads)], axis=1)
        ordered[which, 0] = moved_rows(to_output, together)
        stores[which].start()
    for store in stores:
        store.wait()


def local(ranks, n_ctx, queries, keys, values, grad_out, clip_tokens, text_tokens, anchor_rank, send_block):
    rows, width = queries.shape[1:]
    heads = width // DH
    total = rows * n_ctx
    groups = n_ctx // PARTS
    block_rows = MOVE * PARTS
    spread = rows * PARTS
    outside = pl.BlockSpec(memory_space=pltpu.HBM)
    blocks = pltpu.VMEM((2, ranks, block_rows, width // PARTS), BF16)
    head_blocks = pltpu.VMEM((2, heads, rows, DH), BF16)
    place_blocks = pltpu.VMEM((2, n_ctx, rows, DH), BF16)
    rank_blocks = pltpu.VMEM((2, ranks, groups, block_rows, DH), BF16)
    returned = pl.pallas_call(
        functools.partial(kernel, ranks, n_ctx, heads),
        out_shape=jax.ShapeDtypeStruct((2, heads, rows, DH), BF16),
        in_specs=[outside] * 8,
        out_specs=outside,
        scratch_shapes=[
            pltpu.SMEM(clip_tokens.shape, jnp.int32),
            pltpu.SMEM(text_tokens.shape, jnp.int32),
            pltpu.VMEM(anchor_rank.shape, jnp.int32),
            pltpu.VMEM(send_block.shape, jnp.int32),
            pltpu.VMEM((4,) + queries.shape, BF16),
            blocks,
            blocks,
            head_blocks,
            place_blocks,
            head_blocks,
            place_blocks,
            rank_blocks,
            rank_blocks,
            pltpu.VMEM((2, groups, spread, DH), BF16),
            pltpu.VMEM((groups, spread, total), BF16),
            pltpu.VMEM((total, 2 * DH), BF16),
            pltpu.VMEM((groups, spread, DH), F32),
            pltpu.VMEM((groups, spread, DH), F32),
            place_blocks,
            pltpu.SemaphoreType.DMA((8,)),
            pltpu.SemaphoreType.DMA((4,)),
            pltpu.SemaphoreType.DMA((4,)),
            pltpu.SemaphoreType.DMA((4,)),
            pltpu.SemaphoreType.DMA((4,)),
            pltpu.SemaphoreType.DMA((2,)),
            pltpu.SemaphoreType.DMA((2,)),
        ],
        compiler_params=pltpu.CompilerParams(
            collective_id=0, has_side_effects=True, vmem_limit_bytes=58 * 1024 * 1024
        ),
        cost_estimate=pl.CostEstimate(
            flops=8 * total * total * DH, bytes_accessed=12 * rows * width, transcendentals=total * total
        ),
    )(clip_tokens, text_tokens, anchor_rank, send_block, keys, queries, values, grad_out)
    shape = jax.ShapeDtypeStruct(queries.shape, BF16)
    return pl.pallas_call(
        functools.partial(in_slot_order, heads),
        out_shape=(shape, shape),
        in_specs=[outside, outside],
        out_specs=(outside, outside),
        scratch_shapes=[
            pltpu.VMEM(anchor_rank.shape, jnp.int32),
            pltpu.VMEM((2, heads, rows, DH), BF16),
            pltpu.VMEM((2,) + queries.shape, BF16),
            pltpu.SemaphoreType.DMA((3,)),
            pltpu.SemaphoreType.DMA((2,)),
        ],
        compiler_params=pltpu.CompilerParams(vmem_limit_bytes=58 * 1024 * 1024),
        cost_estimate=pl.CostEstimate(
            flops=4 * rows * rows * width, bytes_accessed=8 * rows * width, transcendentals=0
        ),
    )(anchor_rank, returned)


def solution(mesh):
    split = P("dp", "ctx", None)
    return jax.shard_map(
        functools.partial(local, mesh.shape["dp"], mesh.shape["ctx"]),
        mesh=mesh,
        in_specs=(split, split, split, split, P(), P(), split, split),
        out_specs=(split, split),
        check_vma=False,
    )
```

```python
import functools

import jax
import jax.numpy as jnp
from jax import lax
from jax.experimental import pallas as pl
from jax.experimental.pallas import tpu as pltpu
from jax.sharding import PartitionSpec as P

DH = 128
TEXT = 256
MOVE = 4
PARTS = 4
LOG2E = 1.4426950408889634
KINDS = 4
MESH = pl.DeviceIdType.MESH
F32 = jnp.float32
BF16 = jnp.bfloat16
LAST_DIMS = (((1,), (1,)), ((), ()))


def one_hot(size, source):
    columns = lax.broadcasted_iota(jnp.int32, (source.shape[0], size), 1)
    return (columns == source).astype(F32).astype(BF16)


def looked_up(table, index):
    count = table.shape[1]
    lanes = lax.broadcasted_iota(jnp.int32, (index.shape[0], count), 1)
    spread = jnp.broadcast_to(table, (index.shape[0], count))
    return jnp.sum(jnp.where(lanes == index, spread, 0), axis=1, keepdims=True)


def moved_rows(order, array):
    return jnp.dot(order, array, preferred_element_type=F32).astype(BF16)


def all_bytes(ref, sem):
    pltpu.make_async_copy(ref, ref, sem).wait()


def idle_places(kind):
    plane = 1 - kind // 2
    core = lax.rem(kind, 2)
    first = 2 * (plane + 2 * core)
    second = 2 * (plane + 2 * (1 - core)) + 1
    return jnp.minimum(first, second), jnp.maximum(first, second)


def owner_of(kind, head):
    low, high = idle_places(kind)
    inner = lax.rem(head, 6)
    inner = inner + jnp.where(inner >= low, 1, 0)
    inner = inner + jnp.where(inner >= high, 1, 0)
    return head // 6 * 8 + inner


def head_at(kind, place):
    low, high = idle_places(kind)
    inner = lax.rem(place, 8)
    head = place // 8 * 6 + inner - jnp.where(inner > low, 1, 0) - jnp.where(inner > high, 1, 0)
    return head, (inner != low) & (inner != high)


def idle_kind(place):
    plane, side = lax.rem(place // 2, 4), lax.rem(place, 2)
    return (1 - lax.rem(plane, 2)) * 2 + lax.rem(plane // 2 + side, 2)


def kernel(
    ranks, n_ctx, heads,
    clip_hbm, text_hbm, anchor_hbm, send_hbm, k_hbm, q_hbm, v_hbm, g_hbm,
    returned,
    clip_ref, text_ref, anchor_ref, send_ref, loaded,
    packed, landed, by_head, head_rows,
    columns, column_rows, to_ranks, from_ranks, query_rows,
    expos, ones_v, output, scale_row, results,
    load_sem, dp_send, dp_recv, ctx_send, ctx_recv, back_send, back_recv,
):
    rows = ranks * MOVE
    total = rows * n_ctx
    part_width = heads * DH // PARTS
    part_heads = heads // PARTS
    groups = n_ctx // PARTS
    spread = rows * PARTS
    block_rows = MOVE * PARTS
    rank = lax.axis_index("dp")
    place = lax.axis_index("ctx")
    kind = lax.rem(rank, KINDS)
    my_head, owns = head_at(kind, place)
    idle = idle_kind(place)
    per_kind = ranks // KINDS
    kind_rows = rows // KINDS
    factor = DH ** (-0.5)

    loads = [
        pltpu.make_async_copy(source, target, load_sem.at[index])
        for index, (source, target) in enumerate((
            (send_hbm, send_ref), (anchor_hbm, anchor_ref),
            (k_hbm, loaded.at[0]), (q_hbm, loaded.at[1]), (v_hbm, loaded.at[2]), (g_hbm, loaded.at[3]),
            (clip_hbm, clip_ref), (text_hbm, text_ref),
        ))
    ]
    barrier = pltpu.get_barrier_semaphore()

    def greet_rank(step, _):
        peer = lax.rem(rank + step, ranks)
        pl.semaphore_signal(barrier, inc=1, device_id=(peer, place), device_id_type=MESH)
        return 0

    def greet_place(step, _):
        peer = lax.rem(place + step, n_ctx)
        pl.semaphore_signal(barrier, inc=1, device_id=(rank, peer), device_id_type=MESH)
        return 0

    for index in (0, 3, 2, 5, 4, 1, 6, 7):
        loads[index].start()
    for step in range(1, ranks):
        greet_rank(step, 0)
    for step in range(1, n_ctx):
        greet_place(step, 0)

    loads[0].wait()
    line = lax.broadcasted_iota(jnp.int32, (spread, 1), 0)
    short = lax.broadcasted_iota(jnp.int32, (rows, 1), 0)
    inner = lax.rem(line, MOVE)
    send_table = send_ref[0]

    def pack_blocks(which, array):
        stacked = jnp.concatenate(
            [array[:, part * part_width:(part + 1) * part_width] for part in range(PARTS)], axis=0
        )
        packed[which] = moved_rows(to_send, stacked).reshape(ranks, block_rows, part_width)

    def pack_columns(which, array):
        ordered = moved_rows(to_clip, array)
        for head in range(heads):
            columns[which, head] = ordered[:, head * DH:(head + 1) * DH]

    def far_and_near(step):
        return lax.rem(per_kind // 2 + 3 * step, per_kind)

    def head_in_turn(step):
        return lax.rem(place * heads // n_ctx + 5 * step, heads)

    def over_ranks(source, target, which):
        pltpu.make_async_copy(source.at[rank], target.at[rank], dp_recv.at[which]).start()

        def send_to(peer):
            pltpu.make_async_remote_copy(
                src_ref=source.at[peer],
                dst_ref=target.at[rank],
                send_sem=dp_send.at[which],
                recv_sem=dp_recv.at[which],
                device_id=(peer, place),
                device_id_type=MESH,
            ).start()

        def send_row(step, _):
            row = lax.rem(rank // KINDS + far_and_near(step), per_kind)
            for target_kind in range(KINDS):
                peer = row * KINDS + target_kind

                @pl.when(peer != rank)
                def _(peer=peer):
                    send_to(peer)

            return 0

        lax.fori_loop(0, per_kind, send_row, 0)

    def over_heads(source, target, which):
        def send_head(step, _):
            head = head_in_turn(step)
            owner = owner_of(kind, head)

            @pl.when(owner == place)
            def _():
                pltpu.make_async_copy(source.at[head], target.at[place], ctx_recv.at[which]).start()

            @pl.when(owner != place)
            def _():
                pltpu.make_async_remote_copy(
                    src_ref=source.at[head],
                    dst_ref=target.at[place],
                    send_sem=ctx_send.at[which],
                    recv_sem=ctx_recv.at[which],
                    device_id=(rank, owner),
                    device_id_type=MESH,
                ).start()

            return 0

        lax.fori_loop(0, heads, send_head, 0)

    def columns_to_owners(which):
        def send_head(step, _):
            head = head_in_turn(step)
            for target_kind in range(KINDS):
                owner = owner_of(target_kind, head)
                part = pl.ds(target_kind * kind_rows, kind_rows)
                source = columns.at[which, head, part]
                target = column_rows.at[which, place, part]

                @pl.when(owner == place)
                def _(source=source, target=target):
                    pltpu.make_async_copy(source, target, ctx_recv.at[2 + which]).start()

                @pl.when(owner != place)
                def _(source=source, target=target, owner=owner):
                    pltpu.make_async_remote_copy(
                        src_ref=source,
                        dst_ref=target,
                        send_sem=ctx_send.at[2 + which],
                        recv_sem=ctx_recv.at[2 + which],
                        device_id=(rank, owner),
                        device_id_type=MESH,
                    ).start()

            return 0

        lax.fori_loop(0, heads, send_head, 0)

    def columns_to_ranks(which):
        def send_row(step, _):
            row = lax.rem(rank // KINDS + far_and_near(step), per_kind)
            for target_kind in range(KINDS):
                peer = row * KINDS + target_kind
                source = to_ranks.at[which, target_kind * per_kind + row]
                target = from_ranks.at[which, rank]

                @pl.when((target_kind != idle) & (peer == rank))
                def _(source=source, target=target):
                    pltpu.make_async_copy(source, target, dp_recv.at[2 + which]).start()

                @pl.when((target_kind != idle) & (peer != rank))
                def _(source=source, target=target, peer=peer):
                    pltpu.make_async_remote_copy(
                        src_ref=source,
                        dst_ref=target,
                        send_sem=dp_send.at[2 + which],
                        recv_sem=dp_recv.at[2 + which],
                        device_id=(peer, place),
                        device_id_type=MESH,
                    ).start()

            return 0

        lax.fori_loop(0, per_kind, send_row, 0)

    def to_place(which, target):
        source = results.at[which, target]

        @pl.when(target == place)
        def _():
            pltpu.make_async_copy(source, returned.at[which, my_head], back_recv.at[which]).start()

        @pl.when(target != place)
        def _():
            pltpu.make_async_remote_copy(
                src_ref=source,
                dst_ref=returned.at[which, my_head],
                send_sem=back_send.at[which],
                recv_sem=back_recv.at[which],
                device_id=(rank, target),
                device_id_type=MESH,
            ).start()

    def scatter_blocks(which):
        all_bytes(landed.at[which], dp_recv.at[which])
        ordered = moved_rows(to_slot, landed[which].reshape(spread, part_width))
        for head in range(heads):
            part, column = head // part_heads, head % part_heads
            by_head[which, head] = ordered[part * rows:(part + 1) * rows, column * DH:(column + 1) * DH]
        over_heads(by_head.at[which], head_rows.at[which], which)

    def scatter_columns(which):
        all_bytes(column_rows.at[which, pl.ds(0, n_ctx // KINDS * (KINDS - 1))], ctx_recv.at[2 + which])
        gathered = jnp.concatenate(
            [
                column_rows[which, group * PARTS:(group + 1) * PARTS].reshape(spread, DH)
                for group in range(groups)
            ],
            axis=1,
        )
        mixed = moved_rows(mix, gathered)
        for group in range(groups):
            piece = mixed[:, group * DH:(group + 1) * DH]
            to_ranks[which, :, group] = piece.reshape(ranks, block_rows, DH)
        columns_to_ranks(which)

    def take_columns(which):
        all_bytes(from_ranks.at[which], dp_recv.at[2 + which])
        gathered = jnp.concatenate(
            [from_ranks[which, :, group].reshape(spread, DH) for group in range(groups)], axis=1
        )
        unmixed = moved_rows(unmix, gathered)
        for group in range(groups):
            query_rows[which, group] = unmixed[:, group * DH:(group + 1) * DH]

    clip = lax.rem(short // MOVE, per_kind) * KINDS + short // kind_rows
    to_clip = one_hot(rows, looked_up(send_table, clip) * MOVE + lax.rem(short, MOVE))
    loads[3].wait()
    pack_columns(0, loaded[1, 0])
    pl.semaphore_wait(barrier, ranks - 1 + n_ctx - 1)
    columns_to_owners(0)
    block = looked_up(send_table, line // block_rows)
    to_send = one_hot(spread, lax.rem(line // MOVE, PARTS) * rows + block * MOVE + inner)
    loads[2].wait()
    pack_blocks(0, loaded[0, 0])
    over_ranks(packed.at[0], landed.at[0], 0)
    loads[5].wait()
    pack_columns(1, loaded[3, 0])
    columns_to_owners(1)
    loads[4].wait()
    pack_blocks(1, loaded[2, 0])
    over_ranks(packed.at[1], landed.at[1], 1)
    loads[6].wait()
    loads[7].wait()

    for which in range(2):
        column_rows[which, :, pl.ds(pl.multiple_of(idle * kind_rows, kind_rows), kind_rows)] = jnp.zeros(
            (n_ctx, kind_rows, DH), BF16
        )

    loads[1].wait()
    anchor_table = anchor_ref[0]
    origin = looked_up(anchor_table, lax.rem(line, rows) // MOVE)
    to_slot = one_hot(spread, origin * block_rows + (line // rows) * MOVE + inner)
    mix = one_hot(spread, lax.rem(line // MOVE, PARTS) * rows + (line // block_rows) * MOVE + inner)
    unmix = one_hot(spread, (lax.rem(line, rows) // MOVE) * block_rows + (line // rows) * MOVE + inner)


    scatter_blocks(0)
    scatter_columns(0)
    scatter_blocks(1)
    scatter_columns(1)

    @pl.when(owns)
    def _():
        all_bytes(head_rows.at[0], ctx_recv.at[0])
        take_columns(0)
        clip_len = clip_ref[rank]
        text_len = text_ref[rank]
        spot = lax.broadcasted_iota(jnp.int32, (1, total), 1)
        alive = (spot < clip_len) | ((spot >= total - TEXT) & (spot < total - TEXT + text_len))
        bias = jnp.where(alive, 0.0, -jnp.inf).astype(F32)

        def weigh(group, _):
            scores = lax.dot_general(
                query_rows[0, group], head_rows[0].reshape(total, DH), LAST_DIMS, preferred_element_type=F32
            ) + bias
            peak = jnp.max(scores, axis=1, keepdims=True)
            expos[group] = jnp.exp2((scores - peak) * (factor * LOG2E)).astype(BF16)
            return 0

        def forward(step, _):
            group = lax.rem(place // PARTS + step, groups)
            summed = jnp.dot(expos[group], ones_v[...], preferred_element_type=F32)
            inverse = 1.0 / summed[:, DH:]
            result = summed[:, :DH] * inverse
            scale_row[group] = inverse * factor
            output[group] = result
            results[0, pl.ds(group * PARTS, PARTS)] = result.astype(BF16).reshape(PARTS, rows, DH)
            for part in range(PARTS):
                to_place(0, group * PARTS + part)
            return 0

        def backward(step, _):
            group = lax.rem(place // PARTS + step, groups)
            cotangent = query_rows[1, group]
            slopes = lax.dot_general(
                cotangent, head_rows[1].reshape(total, DH), LAST_DIMS, preferred_element_type=F32
            )
            drift = jnp.sum(cotangent.astype(F32) * output[group], axis=1, keepdims=True)
            mixed = (expos[group].astype(F32) * (slopes - drift)).astype(BF16)
            grads = jnp.dot(mixed, head_rows[0].reshape(total, DH), preferred_element_type=F32)
            result = (grads * scale_row[group]).astype(BF16)
            results[1, pl.ds(group * PARTS, PARTS)] = result.reshape(PARTS, rows, DH)
            for part in range(PARTS):
                to_place(1, group * PARTS + part)
            return 0

        lax.fori_loop(0, groups, weigh, 0)
        all_bytes(head_rows.at[1], ctx_recv.at[1])
        ones_v[:, :DH] = head_rows[1].reshape(total, DH)
        ones_v[:, DH:] = jnp.ones((total, DH), BF16)
        lax.fori_loop(0, groups, forward, 0)
        take_columns(1)
        lax.fori_loop(0, groups, backward, 0)

    for which in range(2):
        all_bytes(returned.at[which], back_recv.at[which])

    for which in range(2):
        all_bytes(packed.at[which, pl.ds(0, ranks - 1)], dp_send.at[which])
        all_bytes(columns.at[which, pl.ds(0, heads - 1)], ctx_send.at[2 + which])
        all_bytes(columns.at[which, 0, pl.ds(0, kind_rows)], ctx_send.at[2 + which])

    @pl.when(owns)
    def _():
        for which in range(2):
            all_bytes(by_head.at[which, pl.ds(0, heads - 1)], ctx_send.at[which])
            all_bytes(to_ranks.at[which, pl.ds(0, (KINDS - 1) * per_kind - 1)], dp_send.at[2 + which])
            all_bytes(results.at[which, pl.ds(0, n_ctx - 1)], back_send.at[which])

    @pl.when(jnp.logical_not(owns))
    def _():
        for which in range(2):
            all_bytes(by_head.at[which], ctx_send.at[which])
            all_bytes(to_ranks.at[which, pl.ds(0, (KINDS - 1) * per_kind)], dp_send.at[2 + which])


def in_slot_order(heads, anchor_hbm, returned_hbm, out_hbm, grad_hbm, anchor_ref, returned, ordered, load_sem, store_sem):
    rows = returned.shape[2]
    loads = [
        pltpu.make_async_copy(anchor_hbm, anchor_ref, load_sem.at[2]),
        pltpu.make_async_copy(returned_hbm.at[0], returned.at[0], load_sem.at[0]),
        pltpu.make_async_copy(returned_hbm.at[1], returned.at[1], load_sem.at[1]),
    ]
    stores = [
        pltpu.make_async_copy(ordered.at[0], out_hbm, store_sem.at[0]),
        pltpu.make_async_copy(ordered.at[1], grad_hbm, store_sem.at[1]),
    ]
    for load in loads:
        load.start()
    loads[0].wait()
    line = lax.broadcasted_iota(jnp.int32, (rows, 1), 0)
    to_output = one_hot(rows, looked_up(anchor_ref[0], line // MOVE) * MOVE + lax.rem(line, MOVE))
    for which in range(2):
        loads[1 + which].wait()
        together = jnp.concatenate([returned[which, head] for head in range(heads)], axis=1)
        ordered[which, 0] = moved_rows(to_output, together)
        stores[which].start()
    for store in stores:
        store.wait()


def local(ranks, n_ctx, queries, keys, values, grad_out, clip_tokens, text_tokens, anchor_rank, send_block):
    rows, width = queries.shape[1:]
    heads = width // DH
    total = rows * n_ctx
    groups = n_ctx // PARTS
    block_rows = MOVE * PARTS
    spread = rows * PARTS
    outside = pl.BlockSpec(memory_space=pltpu.HBM)
    blocks = pltpu.VMEM((2, ranks, block_rows, width // PARTS), BF16)
    head_blocks = pltpu.VMEM((2, heads, rows, DH), BF16)
    place_blocks = pltpu.VMEM((2, n_ctx, rows, DH), BF16)
    rank_blocks = pltpu.VMEM((2, ranks, groups, block_rows, DH), BF16)
    returned = pl.pallas_call(
        functools.partial(kernel, ranks, n_ctx, heads),
        out_shape=jax.ShapeDtypeStruct((2, heads, rows, DH), BF16),
        in_specs=[outside] * 8,
        out_specs=outside,
        scratch_shapes=[
            pltpu.SMEM(clip_tokens.shape, jnp.int32),
            pltpu.SMEM(text_tokens.shape, jnp.int32),
            pltpu.VMEM(anchor_rank.shape, jnp.int32),
            pltpu.VMEM(send_block.shape, jnp.int32),
            pltpu.VMEM((4,) + queries.shape, BF16),
            blocks,
            blocks,
            head_blocks,
            place_blocks,
            head_blocks,
            place_blocks,
            rank_blocks,
            rank_blocks,
            pltpu.VMEM((2, groups, spread, DH), BF16),
            pltpu.VMEM((groups, spread, total), BF16),
            pltpu.VMEM((total, 2 * DH), BF16),
            pltpu.VMEM((groups, spread, DH), F32),
            pltpu.VMEM((groups, spread, DH), F32),
            place_blocks,
            pltpu.SemaphoreType.DMA((8,)),
            pltpu.SemaphoreType.DMA((4,)),
            pltpu.SemaphoreType.DMA((4,)),
            pltpu.SemaphoreType.DMA((4,)),
            pltpu.SemaphoreType.DMA((4,)),
            pltpu.SemaphoreType.DMA((2,)),
            pltpu.SemaphoreType.DMA((2,)),
        ],
        compiler_params=pltpu.CompilerParams(
            collective_id=0, has_side_effects=True, vmem_limit_bytes=58 * 1024 * 1024
        ),
        cost_estimate=pl.CostEstimate(
            flops=8 * total * total * DH, bytes_accessed=12 * rows * width, transcendentals=total * total
        ),
    )(clip_tokens, text_tokens, anchor_rank, send_block, keys, queries, values, grad_out)
    shape = jax.ShapeDtypeStruct(queries.shape, BF16)
    return pl.pallas_call(
        functools.partial(in_slot_order, heads),
        out_shape=(shape, shape),
        in_specs=[outside, outside],
        out_specs=(outside, outside),
        scratch_shapes=[
            pltpu.VMEM(anchor_rank.shape, jnp.int32),
            pltpu.VMEM((2, heads, rows, DH), BF16),
            pltpu.VMEM((2,) + queries.shape, BF16),
            pltpu.SemaphoreType.DMA((3,)),
            pltpu.SemaphoreType.DMA((2,)),
        ],
        compiler_params=pltpu.CompilerParams(vmem_limit_bytes=58 * 1024 * 1024),
        cost_estimate=pl.CostEstimate(
            flops=4 * rows * rows * width, bytes_accessed=8 * rows * width, transcendentals=0
        ),
    )(anchor_rank, returned)


def solution(mesh):
    split = P("dp", "ctx", None)
    return jax.shard_map(
        functools.partial(local, mesh.shape["dp"], mesh.shape["ctx"]),
        mesh=mesh,
        in_specs=(split, split, split, split, P(), P(), split, split),
        out_specs=(split, split),
        check_vma=False,
    )
```

```python
import functools

import jax
import jax.numpy as jnp
from jax import lax
from jax.experimental import pallas as pl
from jax.experimental.pallas import tpu as pltpu
from jax.sharding import PartitionSpec as P

DH = 128
TEXT = 256
MOVE = 4
PARTS = 4
LOG2E = 1.4426950408889634
KINDS = 4
MESH = pl.DeviceIdType.MESH
F32 = jnp.float32
BF16 = jnp.bfloat16
LAST_DIMS = (((1,), (1,)), ((), ()))


def one_hot(size, source):
    columns = lax.broadcasted_iota(jnp.int32, (source.shape[0], size), 1)
    return (columns == source).astype(F32).astype(BF16)


def looked_up(table, index):
    count = table.shape[1]
    lanes = lax.broadcasted_iota(jnp.int32, (index.shape[0], count), 1)
    spread = jnp.broadcast_to(table, (index.shape[0], count))
    return jnp.sum(jnp.where(lanes == index, spread, 0), axis=1, keepdims=True)


def moved_rows(order, array):
    return jnp.dot(order, array, preferred_element_type=F32).astype(BF16)


def all_bytes(ref, sem):
    pltpu.make_async_copy(ref, ref, sem).wait()


def idle_places(kind):
    plane = 1 - kind // 2
    core = lax.rem(kind, 2)
    first = 2 * (plane + 2 * core)
    second = 2 * (plane + 2 * (1 - core)) + 1
    return jnp.minimum(first, second), jnp.maximum(first, second)


def owner_of(kind, head):
    low, high = idle_places(kind)
    inner = lax.rem(head, 6)
    inner = inner + jnp.where(inner >= low, 1, 0)
    inner = inner + jnp.where(inner >= high, 1, 0)
    return head // 6 * 8 + inner


def head_at(kind, place):
    low, high = idle_places(kind)
    inner = lax.rem(place, 8)
    head = place // 8 * 6 + inner - jnp.where(inner > low, 1, 0) - jnp.where(inner > high, 1, 0)
    return head, (inner != low) & (inner != high)


def idle_kind(place):
    plane, side = lax.rem(place // 2, 4), lax.rem(place, 2)
    return (1 - lax.rem(plane, 2)) * 2 + lax.rem(plane // 2 + side, 2)


def kernel(
    ranks, n_ctx, heads,
    clip_hbm, text_hbm, anchor_hbm, send_hbm, k_hbm, q_hbm, v_hbm, g_hbm,
    returned,
    clip_ref, text_ref, anchor_ref, send_ref, loaded,
    packed, landed, by_head, head_rows,
    columns, column_rows, to_ranks, from_ranks, query_rows,
    expos, ones_v, output, scale_row, results,
    load_sem, dp_send, dp_recv, ctx_send, ctx_recv, back_send, back_recv,
):
    rows = ranks * MOVE
    total = rows * n_ctx
    part_width = heads * DH // PARTS
    part_heads = heads // PARTS
    groups = n_ctx // PARTS
    spread = rows * PARTS
    block_rows = MOVE * PARTS
    rank = lax.axis_index("dp")
    place = lax.axis_index("ctx")
    kind = lax.rem(rank, KINDS)
    my_head, owns = head_at(kind, place)
    idle = idle_kind(place)
    per_kind = ranks // KINDS
    kind_rows = rows // KINDS
    factor = DH ** (-0.5)

    loads = [
        pltpu.make_async_copy(source, target, load_sem.at[index])
        for index, (source, target) in enumerate((
            (send_hbm, send_ref), (anchor_hbm, anchor_ref),
            (k_hbm, loaded.at[0]), (q_hbm, loaded.at[1]), (v_hbm, loaded.at[2]), (g_hbm, loaded.at[3]),
            (clip_hbm, clip_ref), (text_hbm, text_ref),
        ))
    ]
    barrier = pltpu.get_barrier_semaphore()

    def greet_rank(step, _):
        peer = lax.rem(rank + step, ranks)
        pl.semaphore_signal(barrier, inc=1, device_id=(peer, place), device_id_type=MESH)
        return 0

    def greet_place(step, _):
        peer = lax.rem(place + step, n_ctx)
        pl.semaphore_signal(barrier, inc=1, device_id=(rank, peer), device_id_type=MESH)
        return 0

    for index in (0, 3, 2, 5, 4, 1, 6, 7):
        loads[index].start()
    for step in range(1, ranks):
        greet_rank(step, 0)
    for step in range(1, n_ctx):
        greet_place(step, 0)

    loads[0].wait()
    line = lax.broadcasted_iota(jnp.int32, (spread, 1), 0)
    short = lax.broadcasted_iota(jnp.int32, (rows, 1), 0)
    inner = lax.rem(line, MOVE)
    send_table = send_ref[0]

    def pack_blocks(which, array):
        stacked = jnp.concatenate(
            [array[:, part * part_width:(part + 1) * part_width] for part in range(PARTS)], axis=0
        )
        packed[which] = moved_rows(to_send, stacked).reshape(ranks, block_rows, part_width)

    def pack_columns(which, array):
        ordered = moved_rows(to_clip, array)
        for head in range(heads):
            columns[which, head] = ordered[:, head * DH:(head + 1) * DH]

    def far_and_near(step):
        return lax.rem(per_kind // 2 + 3 * step, per_kind)

    def head_in_turn(step):
        return lax.rem(place * heads // n_ctx + 5 * step, heads)

    def over_ranks(source, target, which):
        pltpu.make_async_copy(source.at[rank], target.at[rank], dp_recv.at[which]).start()

        def send_to(peer):
            pltpu.make_async_remote_copy(
                src_ref=source.at[peer],
                dst_ref=target.at[rank],
                send_sem=dp_send.at[which],
                recv_sem=dp_recv.at[which],
                device_id=(peer, place),
                device_id_type=MESH,
            ).start()

        def send_row(step, _):
            row = lax.rem(rank // KINDS + far_and_near(step), per_kind)
            for target_kind in range(KINDS):
                peer = row * KINDS + target_kind

                @pl.when(peer != rank)
                def _(peer=peer):
                    send_to(peer)

            return 0

        lax.fori_loop(0, per_kind, send_row, 0)

    def over_heads(source, target, which):
        def send_head(step, _):
            head = head_in_turn(step)
            owner = owner_of(kind, head)

            @pl.when(owner == place)
            def _():
                pltpu.make_async_copy(source.at[head], target.at[place], ctx_recv.at[which]).start()

            @pl.when(owner != place)
            def _():
                pltpu.make_async_remote_copy(
                    src_ref=source.at[head],
                    dst_ref=target.at[place],
                    send_sem=ctx_send.at[which],
                    recv_sem=ctx_recv.at[which],
                    device_id=(rank, owner),
                    device_id_type=MESH,
                ).start()

            return 0

        lax.fori_loop(0, heads, send_head, 0)

    def columns_to_owners(which):
        def send_head(step, _):
            head = head_in_turn(step)
            for target_kind in range(KINDS):
                owner = owner_of(target_kind, head)
                part = pl.ds(target_kind * kind_rows, kind_rows)
                source = columns.at[which, head, part]
                target = column_rows.at[which, place, part]

                @pl.when(owner == place)
                def _(source=source, target=target):
                    pltpu.make_async_copy(source, target, ctx_recv.at[2 + which]).start()

                @pl.when(owner != place)
                def _(source=source, target=target, owner=owner):
                    pltpu.make_async_remote_copy(
                        src_ref=source,
                        dst_ref=target,
                        send_sem=ctx_send.at[2 + which],
                        recv_sem=ctx_recv.at[2 + which],
                        device_id=(rank, owner),
                        device_id_type=MESH,
                    ).start()

            return 0

        lax.fori_loop(0, heads, send_head, 0)

    def columns_to_ranks(which):
        def send_row(step, _):
            row = lax.rem(rank // KINDS + far_and_near(step), per_kind)
            for target_kind in range(KINDS):
                peer = row * KINDS + target_kind
                source = to_ranks.at[which, target_kind * per_kind + row]
                target = from_ranks.at[which, rank]

                @pl.when((target_kind != idle) & (peer == rank))
                def _(source=source, target=target):
                    pltpu.make_async_copy(source, target, dp_recv.at[2 + which]).start()

                @pl.when((target_kind != idle) & (peer != rank))
                def _(source=source, target=target, peer=peer):
                    pltpu.make_async_remote_copy(
                        src_ref=source,
                        dst_ref=target,
                        send_sem=dp_send.at[2 + which],
                        recv_sem=dp_recv.at[2 + which],
                        device_id=(peer, place),
                        device_id_type=MESH,
                    ).start()

            return 0

        lax.fori_loop(0, per_kind, send_row, 0)

    def to_place(which, target):
        source = results.at[which, target]

        @pl.when(target == place)
        def _():
            pltpu.make_async_copy(source, returned.at[which, my_head], back_recv.at[which]).start()

        @pl.when(target != place)
        def _():
            pltpu.make_async_remote_copy(
                src_ref=source,
                dst_ref=returned.at[which, my_head],
                send_sem=back_send.at[which],
                recv_sem=back_recv.at[which],
                device_id=(rank, target),
                device_id_type=MESH,
            ).start()

    def scatter_blocks(which):
        all_bytes(landed.at[which], dp_recv.at[which])
        ordered = moved_rows(to_slot, landed[which].reshape(spread, part_width))
        for head in range(heads):
            part, column = head // part_heads, head % part_heads
            by_head[which, head] = ordered[part * rows:(part + 1) * rows, column * DH:(column + 1) * DH]
        over_heads(by_head.at[which], head_rows.at[which], which)

    def scatter_columns(which):
        all_bytes(column_rows.at[which, pl.ds(0, n_ctx // KINDS * (KINDS - 1))], ctx_recv.at[2 + which])
        gathered = jnp.concatenate(
            [
                column_rows[which, group * PARTS:(group + 1) * PARTS].reshape(spread, DH)
                for group in range(groups)
            ],
            axis=1,
        )
        mixed = moved_rows(mix, gathered)
        for group in range(groups):
            piece = mixed[:, group * DH:(group + 1) * DH]
            to_ranks[which, :, group] = piece.reshape(ranks, block_rows, DH)
        columns_to_ranks(which)

    def take_columns(which):
        all_bytes(from_ranks.at[which], dp_recv.at[2 + which])
        gathered = jnp.concatenate(
            [from_ranks[which, :, group].reshape(spread, DH) for group in range(groups)], axis=1
        )
        unmixed = moved_rows(unmix, gathered)
        for group in range(groups):
            query_rows[which, group] = unmixed[:, group * DH:(group + 1) * DH]

    clip = lax.rem(short // MOVE, per_kind) * KINDS + short // kind_rows
    to_clip = one_hot(rows, looked_up(send_table, clip) * MOVE + lax.rem(short, MOVE))
    loads[3].wait()
    pack_columns(0, loaded[1, 0])
    pl.semaphore_wait(barrier, ranks - 1 + n_ctx - 1)
    columns_to_owners(0)
    block = looked_up(send_table, line // block_rows)
    to_send = one_hot(spread, lax.rem(line // MOVE, PARTS) * rows + block * MOVE + inner)
    loads[2].wait()
    pack_blocks(0, loaded[0, 0])
    over_ranks(packed.at[0], landed.at[0], 0)
    loads[5].wait()
    pack_columns(1, loaded[3, 0])
    columns_to_owners(1)
    loads[4].wait()
    pack_blocks(1, loaded[2, 0])
    over_ranks(packed.at[1], landed.at[1], 1)
    loads[6].wait()
    loads[7].wait()

    for which in range(2):
        column_rows[which, :, pl.ds(pl.multiple_of(idle * kind_rows, kind_rows), kind_rows)] = jnp.zeros(
            (n_ctx, kind_rows, DH), BF16
        )

    loads[1].wait()
    anchor_table = anchor_ref[0]
    origin = looked_up(anchor_table, lax.rem(line, rows) // MOVE)
    to_slot = one_hot(spread, origin * block_rows + (line // rows) * MOVE + inner)
    mix = one_hot(spread, lax.rem(line // MOVE, PARTS) * rows + (line // block_rows) * MOVE + inner)
    unmix = one_hot(spread, (lax.rem(line, rows) // MOVE) * block_rows + (line // rows) * MOVE + inner)


    scatter_blocks(0)
    scatter_columns(0)
    scatter_blocks(1)
    scatter_columns(1)

    @pl.when(owns)
    def _():
        all_bytes(head_rows.at[0], ctx_recv.at[0])
        take_columns(0)
        clip_len = clip_ref[rank]
        text_len = text_ref[rank]
        spot = lax.broadcasted_iota(jnp.int32, (1, total), 1)
        alive = (spot < clip_len) | ((spot >= total - TEXT) & (spot < total - TEXT + text_len))
        bias = jnp.where(alive, 0.0, -jnp.inf).astype(F32)

        def weigh(group, _):
            scores = lax.dot_general(
                query_rows[0, group], head_rows[0].reshape(total, DH), LAST_DIMS, preferred_element_type=F32
            ) + bias
            peak = jnp.max(scores, axis=1, keepdims=True)
            expos[group] = jnp.exp2((scores - peak) * (factor * LOG2E)).astype(BF16)
            return 0

        def forward(step, _):
            group = lax.rem(place // PARTS + step, groups)
            summed = jnp.dot(expos[group], ones_v[...], preferred_element_type=F32)
            inverse = 1.0 / summed[:, DH:]
            result = summed[:, :DH] * inverse
            scale_row[group] = inverse * factor
            output[group] = result
            results[0, pl.ds(group * PARTS, PARTS)] = result.astype(BF16).reshape(PARTS, rows, DH)
            for part in range(PARTS):
                to_place(0, group * PARTS + part)
            return 0

        def backward(step, _):
            group = lax.rem(place // PARTS + step, groups)
            cotangent = query_rows[1, group]
            slopes = lax.dot_general(
                cotangent, head_rows[1].reshape(total, DH), LAST_DIMS, preferred_element_type=F32
            )
            drift = jnp.sum(cotangent.astype(F32) * output[group], axis=1, keepdims=True)
            mixed = (expos[group].astype(F32) * (slopes - drift)).astype(BF16)
            grads = jnp.dot(mixed, head_rows[0].reshape(total, DH), preferred_element_type=F32)
            result = (grads * scale_row[group]).astype(BF16)
            results[1, pl.ds(group * PARTS, PARTS)] = result.reshape(PARTS, rows, DH)
            for part in range(PARTS):
                to_place(1, group * PARTS + part)
            return 0

        lax.fori_loop(0, groups, weigh, 0)
        all_bytes(head_rows.at[1], ctx_recv.at[1])
        ones_v[:, :DH] = head_rows[1].reshape(total, DH)
        ones_v[:, DH:] = jnp.ones((total, DH), BF16)
        lax.fori_loop(0, groups, forward, 0)
        take_columns(1)
        lax.fori_loop(0, groups, backward, 0)

    for which in range(2):
        all_bytes(returned.at[which], back_recv.at[which])

    for which in range(2):
        all_bytes(packed.at[which, pl.ds(0, ranks - 1)], dp_send.at[which])
        all_bytes(columns.at[which, pl.ds(0, heads - 1)], ctx_send.at[2 + which])
        all_bytes(columns.at[which, 0, pl.ds(0, kind_rows)], ctx_send.at[2 + which])

    @pl.when(owns)
    def _():
        for which in range(2):
            all_bytes(by_head.at[which, pl.ds(0, heads - 1)], ctx_send.at[which])
            all_bytes(to_ranks.at[which, pl.ds(0, (KINDS - 1) * per_kind - 1)], dp_send.at[2 + which])
            all_bytes(results.at[which, pl.ds(0, n_ctx - 1)], back_send.at[which])

    @pl.when(jnp.logical_not(owns))
    def _():
        for which in range(2):
            all_bytes(by_head.at[which], ctx_send.at[which])
            all_bytes(to_ranks.at[which, pl.ds(0, (KINDS - 1) * per_kind)], dp_send.at[2 + which])


def in_slot_order(heads, anchor_hbm, returned_hbm, out_hbm, grad_hbm, anchor_ref, returned, ordered, load_sem, store_sem):
    rows = returned.shape[2]
    half = heads // 2
    pieces = [(which, first) for which in range(2) for first in (0, half)]
    anchor_load = pltpu.make_async_copy(anchor_hbm, anchor_ref, load_sem.at[4])
    anchor_load.start()
    loads, stores = [], []
    for index, (which, first) in enumerate(pieces):
        some = pl.ds(first, half)
        columns = pl.ds(first * DH, half * DH)
        target = (out_hbm, grad_hbm)[which]
        loads.append(
            pltpu.make_async_copy(returned_hbm.at[which, some], returned.at[which, some], load_sem.at[index])
        )
        stores.append(
            pltpu.make_async_copy(ordered.at[which, :, :, columns], target.at[:, :, columns], store_sem.at[index])
        )
        loads[-1].start()
    anchor_load.wait()
    line = lax.broadcasted_iota(jnp.int32, (rows, 1), 0)
    to_output = one_hot(rows, looked_up(anchor_ref[0], line // MOVE) * MOVE + lax.rem(line, MOVE))
    for index, (which, first) in enumerate(pieces):
        loads[index].wait()
        together = jnp.concatenate([returned[which, first + head] for head in range(half)], axis=1)
        ordered[which, 0, :, first * DH:(first + half) * DH] = moved_rows(to_output, together)
        stores[index].start()
    for store in stores:
        store.wait()


def local(ranks, n_ctx, queries, keys, values, grad_out, clip_tokens, text_tokens, anchor_rank, send_block):
    rows, width = queries.shape[1:]
    heads = width // DH
    total = rows * n_ctx
    groups = n_ctx // PARTS
    block_rows = MOVE * PARTS
    spread = rows * PARTS
    outside = pl.BlockSpec(memory_space=pltpu.HBM)
    blocks = pltpu.VMEM((2, ranks, block_rows, width // PARTS), BF16)
    head_blocks = pltpu.VMEM((2, heads, rows, DH), BF16)
    place_blocks = pltpu.VMEM((2, n_ctx, rows, DH), BF16)
    rank_blocks = pltpu.VMEM((2, ranks, groups, block_rows, DH), BF16)
    returned = pl.pallas_call(
        functools.partial(kernel, ranks, n_ctx, heads),
        out_shape=jax.ShapeDtypeStruct((2, heads, rows, DH), BF16),
        in_specs=[outside] * 8,
        out_specs=outside,
        scratch_shapes=[
            pltpu.SMEM(clip_tokens.shape, jnp.int32),
            pltpu.SMEM(text_tokens.shape, jnp.int32),
            pltpu.VMEM(anchor_rank.shape, jnp.int32),
            pltpu.VMEM(send_block.shape, jnp.int32),
            pltpu.VMEM((4,) + queries.shape, BF16),
            blocks,
            blocks,
            head_blocks,
            place_blocks,
            head_blocks,
            place_blocks,
            rank_blocks,
            rank_blocks,
            pltpu.VMEM((2, groups, spread, DH), BF16),
            pltpu.VMEM((groups, spread, total), BF16),
            pltpu.VMEM((total, 2 * DH), BF16),
            pltpu.VMEM((groups, spread, DH), F32),
            pltpu.VMEM((groups, spread, DH), F32),
            place_blocks,
            pltpu.SemaphoreType.DMA((8,)),
            pltpu.SemaphoreType.DMA((4,)),
            pltpu.SemaphoreType.DMA((4,)),
            pltpu.SemaphoreType.DMA((4,)),
            pltpu.SemaphoreType.DMA((4,)),
            pltpu.SemaphoreType.DMA((2,)),
            pltpu.SemaphoreType.DMA((2,)),
        ],
        compiler_params=pltpu.CompilerParams(
            collective_id=0, has_side_effects=True, vmem_limit_bytes=58 * 1024 * 1024
        ),
        cost_estimate=pl.CostEstimate(
            flops=8 * total * total * DH, bytes_accessed=12 * rows * width, transcendentals=total * total
        ),
    )(clip_tokens, text_tokens, anchor_rank, send_block, keys, queries, values, grad_out)
    shape = jax.ShapeDtypeStruct(queries.shape, BF16)
    return pl.pallas_call(
        functools.partial(in_slot_order, heads),
        out_shape=(shape, shape),
        in_specs=[outside, outside],
        out_specs=(outside, outside),
        scratch_shapes=[
            pltpu.VMEM(anchor_rank.shape, jnp.int32),
            pltpu.VMEM((2, heads, rows, DH), BF16),
            pltpu.VMEM((2,) + queries.shape, BF16),
            pltpu.SemaphoreType.DMA((5,)),
            pltpu.SemaphoreType.DMA((4,)),
        ],
        compiler_params=pltpu.CompilerParams(vmem_limit_bytes=58 * 1024 * 1024),
        cost_estimate=pl.CostEstimate(
            flops=4 * rows * rows * width, bytes_accessed=8 * rows * width, transcendentals=0
        ),
    )(anchor_rank, returned)


def solution(mesh):
    split = P("dp", "ctx", None)
    return jax.shard_map(
        functools.partial(local, mesh.shape["dp"], mesh.shape["ctx"]),
        mesh=mesh,
        in_specs=(split, split, split, split, P(), P(), split, split),
        out_specs=(split, split),
        check_vma=False,
    )
```
